128 devices in a mesh: dp: 8 (over z, core), ctx: 16 (over y, x).
Axes of the slice: x: 4, y: 4, z: 4, core: 2. Of those that a mesh axis runs over, the one named last changes fastest.
Arguments:
- tokens: bfloat16 [24576, 1024], P(('dp', 'ctx')), may hold values from -55 to 55
- segments: int32 [8, 3072], P('dp', 'ctx'), may hold values from 0 to 7, never falling along the last dimension, each value on 1 to 1536 neighbouring positions
- w_in: bfloat16 [1024, 4096], replicated, may hold values from -0.1875 to 0.1875
- w_out: bfloat16 [1024, 1024], replicated, may hold values from -0.1875 to 0.1875
- grad_out: bfloat16 [24576, 1024], P(('dp', 'ctx')), may hold values from -24 to 24
Outputs:
- layer_out: bfloat16 [24576, 1024], P(('dp', 'ctx'))
- grad_tokens: bfloat16 [24576, 1024], P(('dp', 'ctx'))
- out_grad: float32 [1024, 1024], P(('dp', 'ctx'))
The draws below stay inside these ranges and needn't reach their ends.
Inputs may be any that keep to these rules, and one draw needn't show every extreme that they name: `segments`: along each stream's stored rows the history number never falls; each of the 8 histories holds 1 to 1536 events, one exactly 1536.
All inputs are finite; a program needn't handle non-finite values.
Results may differ from the reference program's by a relative error of at most 0.008.
Values may be sent and summed in bfloat16 or wider, within the bound.
A program may use at most 128 MiB of HBM per device.

```python
import math
import jax
import jax.numpy as jnp
import numpy as np
from jax import lax

D = 1024
HEADS = 8
HEAD = 128
TOK_DEV = 192
SEGS = 8
SEQ = 3072
LONGEST = 1536
STREAMS = 8
TOKENS = 24576
N_CTX = 16


def draw_tokens(key, part):
    key = jax.random.fold_in(key, 11)
    base_key, row_key, col_key = jax.random.split(key, 3)
    row_scale = jnp.exp(jax.random.uniform(row_key, (TOKENS, 1), jnp.float32, math.log(0.3), math.log(3.0)))
    col_scale = jnp.exp(jax.random.uniform(col_key, (1, D), jnp.float32, math.log(0.3), math.log(3.0)))
    base = jnp.clip(jax.random.normal(base_key, (TOKENS, D), jnp.float32), -6.0, 6.0)
    return (base * row_scale * col_scale).astype(jnp.bfloat16)


def strengthened(array, stream_key, source, target, parts, factor):
    owner, partner = [(jnp.arange(array.shape[position]) // (array.shape[position] // parts)).reshape([-1 if axis == position else 1 for axis in range(array.ndim)]) for position in (source, target)]
    chosen = jax.random.permutation(stream_key, parts)[partner]
    strong = (owner == chosen) | (owner == (partner + parts // 2) % parts)
    return jnp.where(strong, factor * array, array)


def level_of(rng, dims, cuts, least, top_value):
    loudness = 1.0
    for axis_at, shards_of in cuts:
        draws = jax.random.uniform(jax.random.fold_in(jax.random.fold_in(rng, 6), axis_at), (shards_of,), jnp.float32, least / len(cuts), top_value / len(cuts))
        loudness = loudness * jnp.repeat(jnp.exp(draws), dims[axis_at] // shards_of).reshape((-1,) + (1,) * (len(dims) - 1 - axis_at))
    return loudness


def split_up(amount, total, limit, lean):
    portions = [(1 << 20) // math.isqrt(grade ** lean) + 1 for grade in range(2, amount + 1)]
    spare, given = total - limit - (amount - 1), [1] * (amount - 1)
    while spare > 0:
        free = [i for i in range(amount - 1) if given[i] < limit]
        pool, left = sum([portions[i] for i in free]), spare
        for i in free:
            addition = min(limit - given[i], max(1, left * portions[i] // pool), spare)
            given[i] = given[i] + addition
            spare = spare - addition
    return np.array([limit] + given)


def uneven_parts(rng, number_of, total, reach, slope):
    if number_of == 2:
        one = jax.random.randint(rng, (), max(1, total - reach), min(reach, total - 1) + 1)
        return jnp.stack([one, total - one])
    tallies = jnp.asarray(split_up(number_of, total, reach, slope), jnp.int32)
    couples = (number_of - 1) // 2
    giver, sink = tallies[1:1 + 2 * couples:2], tallies[2:2 + 2 * couples:2]
    room = jnp.minimum(giver - 1, reach - sink)
    passed = jax.random.randint(jax.random.fold_in(rng, 1), (couples,), 0, 1 << 20) % (room + 1)
    tallies = tallies.at[1:1 + 2 * couples:2].set(giver - passed).at[2:2 + 2 * couples:2].set(sink + passed)
    return tallies[jax.random.permutation(jax.random.fold_in(rng, 2), number_of)]


def bell_draw(rng, dims, scale, most, shards=(), kind=jnp.bfloat16):
    entries = scale * jax.random.normal(rng, dims, jnp.float32)
    if shards:
        entries = entries * level_of(rng, dims, shards, -0.22, 0.18)
    return jnp.clip(entries, -most, most).astype(kind)


def gaussian_with(stream_key, extent, width, most, cuts, heavy, kind=jnp.bfloat16):
    drawn = width * jax.random.normal(stream_key, extent, jnp.float32)
    if cuts:
        drawn = drawn * level_of(stream_key, extent, cuts, -0.22, 0.18)
    return jnp.clip(strengthened(drawn, jax.random.fold_in(stream_key, 3), *heavy), -most, most).astype(kind)


def setup_inputs(seed: int = 0) -> dict:
    arg_keys = jax.random.split(jax.random.key(seed), 6)
    tokens = draw_tokens(jax.random.fold_in(arg_keys[5], 71), 0)
    segments = jax.vmap(lambda own: jnp.searchsorted(jnp.cumsum(uneven_parts(own, SEGS, SEQ, LONGEST, 2)), jnp.arange(SEQ), side="right"))(jax.random.split(arg_keys[1], STREAMS)).reshape((STREAMS, SEQ)).astype(jnp.int32)
    w_in = bell_draw(arg_keys[2], (D, 4 * D), D ** -0.5, 0.1875)
    w_out = bell_draw(arg_keys[3], (D, D), D ** -0.5, 0.1875)
    grad_out = gaussian_with(arg_keys[4], (TOKENS, D), 1.0, 24.0, ((0, 128),), (0, 1, 128, 5.5))
    return dict(tokens=tokens, segments=segments, w_in=w_in, w_out=w_out, grad_out=grad_out)


EPS = 1e-05

def silu_grad(value):
    sigmoid_v = jax.nn.sigmoid(value)
    return sigmoid_v * (1.0 + value * (1.0 - sigmoid_v))

def norm_rows(matrix):
    average = lax.optimization_barrier(jnp.mean(matrix, axis=-1, keepdims=True))
    centred = matrix - average
    inverse = lax.rsqrt(lax.optimization_barrier(jnp.mean(centred * centred, axis=-1, keepdims=True)) + EPS)
    return (centred * inverse, inverse)

def norm_back(gradient, normed, inverse):
    first = lax.optimization_barrier(jnp.mean(gradient, axis=-1, keepdims=True))
    second = lax.optimization_barrier(jnp.mean(gradient * normed, axis=-1, keepdims=True))
    return (gradient - first - normed * second) * inverse

def to_heads(matrix):
    return matrix.reshape(STREAMS, SEQ, HEADS, HEAD).transpose(0, 2, 1, 3).reshape(STREAMS * HEADS, SEQ, HEAD)

def from_heads(stacked):
    return stacked.reshape(STREAMS, HEADS, SEQ, HEAD).transpose(0, 2, 1, 3).reshape(TOKENS, D)

def stored_places():
    stored = jnp.arange(SEQ, dtype=jnp.int32)
    block = stored // TOK_DEV
    inner = stored % TOK_DEV
    half = TOK_DEV // 2
    return jnp.where(inner < half, block * half + inner, (2 * N_CTX - 1 - block) * half + inner - half).astype(jnp.int32)

def head_scores(query_h, key_h, history):
    score_scale = HEAD ** (-0.5)
    scores = jnp.dot(query_h, key_h.T, preferred_element_type=jnp.float32) * score_scale
    places = stored_places()
    visible = (history[:, None] == history[None, :]) & (places[:, None] >= places[None, :])
    weights = jnp.where(visible, jax.nn.silu(scores), 0.0).astype(jnp.bfloat16)
    return (scores, visible, weights)

def head_forward(operands):
    query_h, key_h, value_h, history = operands
    scores, visible, weights = head_scores(query_h, key_h, history)
    return jnp.dot(weights, value_h, preferred_element_type=jnp.float32)

def head_backward(operands):
    query_h, key_h, value_h, grad_h, history = operands
    score_scale = HEAD ** (-0.5)
    scores, visible, weights = head_scores(query_h, key_h, history)
    grad_weights = jnp.dot(grad_h, value_h.T, preferred_element_type=jnp.float32)
    grad_scores = (jnp.where(visible, grad_weights * silu_grad(scores), 0.0) * score_scale).astype(jnp.bfloat16)
    grad_q = jnp.dot(grad_scores, key_h, preferred_element_type=jnp.float32)
    grad_k = jnp.dot(grad_scores.T, query_h, preferred_element_type=jnp.float32)
    grad_v = jnp.dot(weights.T, grad_h, preferred_element_type=jnp.float32)
    return (grad_q, grad_k, grad_v)

def reference(tokens, segments, w_in, w_out, grad_out):
    xfloat = tokens.astype(jnp.float32)
    normed, inv_x = norm_rows(xfloat)
    normed_b = normed.astype(jnp.bfloat16)
    preact = jnp.dot(normed_b, w_in, preferred_element_type=jnp.float32)
    act = jax.nn.silu(preact).astype(jnp.bfloat16)
    gate_u = act[:, :D]
    values = act[:, D:2 * D]
    queries = act[:, 2 * D:3 * D]
    keys = act[:, 3 * D:]
    histories = jnp.repeat(segments, HEADS, axis=0)
    query_s = to_heads(queries)
    key_s = to_heads(keys)
    value_s = to_heads(values)
    mixed = from_heads(lax.map(head_forward, (query_s, key_s, value_s, histories)))
    mixed_n, inv_o = norm_rows(mixed)
    gated = (mixed_n * gate_u.astype(jnp.float32)).astype(jnp.bfloat16)
    layer_out = (jnp.dot(gated, w_out, preferred_element_type=jnp.float32) + xfloat).astype(jnp.bfloat16)
    out_grad = jnp.dot(grad_out.T, gated, preferred_element_type=jnp.float32) * TOKENS ** (-0.5)
    grad_gated = jnp.dot(grad_out, w_out.T, preferred_element_type=jnp.float32)
    grad_u = grad_gated * mixed_n
    grad_norm = grad_gated * gate_u.astype(jnp.float32)
    grad_mixed = norm_back(grad_norm, mixed_n, inv_o).astype(jnp.bfloat16)
    grad_q, grad_k, grad_v = lax.map(head_backward, (query_s, key_s, value_s, to_heads(grad_mixed), histories))
    grad_all = jnp.concatenate([grad_u, from_heads(grad_v), from_heads(grad_q), from_heads(grad_k)], axis=1)
    grad_pre = (grad_all * silu_grad(preact)).astype(jnp.bfloat16)
    grad_rows = jnp.dot(grad_pre, w_in.T, preferred_element_type=jnp.float32)
    grad_tokens = (grad_out.astype(jnp.float32) + norm_back(grad_rows, normed, inv_x)).astype(jnp.bfloat16)
    return (layer_out, grad_tokens, out_grad)
```

```python
import functools

import jax
import jax.numpy as jnp
from jax import lax
from jax.experimental import pallas as pl
from jax.experimental.pallas import tpu as pltpu
from jax.sharding import PartitionSpec as P

HEADS = 8
HEAD = 128
ROWS = 192
HALF = 96
D = 1024
CTX = 16
EPS = 1e-05
SCALE = HEAD ** (-0.5)
VMEM_LIMIT = 56 * 1024 * 1024
F32 = jnp.float32
BF16 = jnp.bfloat16
K_COL, V_COL, Q_COL, U_COL = 3 * D, D, 2 * D, 0


def silu_and_grad(value):
    half = 0.5 * value
    tanh_h = jnp.tanh(half)
    sigmoid_v = 0.5 + 0.5 * tanh_h
    silu_v = half + half * tanh_h
    return silu_v, sigmoid_v + silu_v * (1.0 - sigmoid_v)


def norm_rows(matrix):
    average = jnp.mean(matrix, axis=-1, keepdims=True)
    centred = matrix - average
    inverse = lax.rsqrt(jnp.mean(centred * centred, axis=-1, keepdims=True) + EPS)
    return centred * inverse, inverse


def norm_back(gradient, normed, inverse):
    first = jnp.mean(gradient, axis=-1, keepdims=True)
    second = jnp.mean(gradient * normed, axis=-1, keepdims=True)
    return (gradient - first - normed * second) * inverse


def dot_nt(left, right):
    return lax.dot_general(left, right, (((1,), (1,)), ((), ())), preferred_element_type=F32)


def dot_tn(left, right):
    return lax.dot_general(left, right, (((0,), (0,)), ((), ())), preferred_element_type=F32)


def dot_nn(left, right):
    return lax.dot_general(left, right, (((1,), (0,)), ((), ())), preferred_element_type=F32)


class Place:
    def __init__(self):
        self.dp = lax.axis_index("dp")
        self.t = lax.axis_index("ctx")
        self.plane = 2 * (self.dp // 2)
        self.core = self.dp % 2
        self.sibling = {"dp": self.plane + 1 - self.core}

    def worker(self, head):
        return self.plane + self.t % 2, self.core * HEADS + head

    def owner(self, i):
        return self.plane + self.t // HEADS, 2 * i + self.core

    def is_me(self, device):
        return (device[0] == self.dp) & (device[1] == self.t)


def ident(device):
    return {"dp": device[0], "ctx": device[1]}


def signal_if_other(place, barrier, device):
    @pl.when(jnp.logical_not(place.is_me(device)))
    def _():
        pl.semaphore_signal(barrier, inc=1, device_id=ident(device))


def start_copy(place, device, src, dst, send_sem, recv_sem):
    mine = place.is_me(device)

    @pl.when(mine)
    def _():
        pltpu.make_async_copy(src, dst, recv_sem).start()

    @pl.when(jnp.logical_not(mine))
    def _():
        pltpu.make_async_remote_copy(
            src, dst, send_sem, recv_sem, device_id=ident(device)
        ).start()


def wait_sent(place, device, src, dst, send_sem, recv_sem):
    @pl.when(jnp.logical_not(place.is_me(device)))
    def _():
        pltpu.make_async_remote_copy(
            src, dst, send_sem, recv_sem, device_id=ident(device)
        ).wait_send()


def wait_arrived(dst, recv_sem):
    pltpu.make_async_copy(dst, dst, recv_sem).wait()


def project_kernel(
    tokens, hist, w_in, q_got, kv_got, hist_all, u_act, preact_out,
    w_buf, normed_buf, pre_buf, u_buf, send_buf, hist_buf,
    w_sem, out_sem, send_sem, recv_sem, fsend, frecv, hsend, hrecv, hfsend, hfrecv,
):
    place = Place()
    chunks = [K_COL, K_COL + 512, V_COL, V_COL + 512, Q_COL, Q_COL + 512, U_COL, U_COL + 512]

    def w_copy(n):
        cols = pl.ds(chunks[n], 512)
        return pltpu.make_async_copy(w_in.at[:, cols], w_buf.at[:, cols], w_sem.at[n])

    for n in range(8):
        w_copy(n).start()

    barrier = pltpu.get_barrier_semaphore()
    for i in range(8):
        signal_if_other(place, barrier, place.owner(i))
    pl.semaphore_signal(barrier, inc=1, device_id=place.sibling)

    normed, _ = norm_rows(tokens[...].astype(F32))
    normed_buf[...] = normed.astype(BF16)
    hist_buf[...] = jnp.zeros_like(hist_buf)
    hist_buf[:, 0:HALF] = hist[:, 0:HALF]
    hist_buf[:, 128 : 128 + HALF] = hist[:, HALF:ROWS]

    self_work = (place.t % 2 == place.core) & (place.t // HEADS == place.core)
    expected = 9 - self_work.astype(jnp.int32)
    pl.semaphore_wait(barrier, expected)

    slot = place.t // 2

    def send_args(kind, head):
        src = send_buf.at[kind, head]
        if kind == 2:
            dst = q_got.at[slot]
        else:
            dst = kv_got.at[kind, :, place.t]
        return place.worker(head), src, dst, send_sem.at[kind, head], recv_sem.at[kind, slot]

    def hist_args(head):
        return (
            place.worker(head), hist_buf, hist_all.at[place.t], hsend.at[head], hrecv.at[slot],
        )

    for head in range(HEADS):
        start_copy(place, *hist_args(head))

    for n in range(8):
        w_copy(n).wait()
        cols = slice(chunks[n], chunks[n] + 512)
        pre = dot_nn(normed_buf[...], w_buf[:, cols])
        pre_buf[:, cols] = pre
        half = 0.5 * pre
        act = (half + half * jnp.tanh(half)).astype(BF16)
        if n < 6:
            kind = n // 2
            for j in range(4):
                head = (n % 2) * 4 + j
                send_buf[kind, head] = act[:, j * 128 : (j + 1) * 128].reshape(2, HALF, HEAD)
                start_copy(place, *send_args(kind, head))
        else:
            u_buf[:, cols] = act

    u_out = pltpu.make_async_copy(u_buf, u_act, out_sem.at[0])
    u_out.start()
    p_out = pltpu.make_async_copy(pre_buf, preact_out, out_sem.at[1])
    p_out.start()

    def forward(kind, i):
        c = 2 * i + place.core
        ref = kv_got.at[kind, :, c]
        return pltpu.make_async_remote_copy(
            ref, ref, fsend.at[kind, i], frecv.at[kind, i], device_id=place.sibling
        )

    def hforward(i):
        c = 2 * i + place.core
        return pltpu.make_async_remote_copy(
            hist_all.at[c], hist_all.at[c], hfsend.at[i], hfrecv.at[i], device_id=place.sibling
        )

    for i in range(8):
        wait_arrived(hist_all.at[2 * i + place.core], hrecv.at[i])
        hforward(i).start()
    for kind in range(2):
        for i in range(8):
            wait_arrived(kv_got.at[kind, :, 2 * i + place.core], recv_sem.at[kind, i])
            forward(kind, i).start()
    for i in range(8):
        wait_arrived(q_got.at[i], recv_sem.at[2, i])
    for i in range(8):
        other = 2 * i + 1 - place.core
        wait_arrived(hist_all.at[other], hfrecv.at[i])
        for kind in range(2):
            wait_arrived(kv_got.at[kind, :, other], frecv.at[kind, i])
    for i in range(8):
        hforward(i).wait_send()
        for kind in range(2):
            forward(kind, i).wait_send()
    for head in range(HEADS):
        wait_sent(place, *hist_args(head))
        for kind in range(3):
            wait_sent(place, *send_args(kind, head))
    u_out.wait()
    p_out.wait()


def project(tokens, hist, w_in):
    any_spec = pl.BlockSpec(memory_space=pl.ANY)
    vmem_spec = pl.BlockSpec(memory_space=pltpu.VMEM)
    dma = pltpu.SemaphoreType.DMA
    return pl.pallas_call(
        project_kernel,
        out_shape=(
            jax.ShapeDtypeStruct((8, 2, HALF, HEAD), BF16),
            jax.ShapeDtypeStruct((2, 2, CTX, HALF, HEAD), BF16),
            jax.ShapeDtypeStruct((CTX, 1, 256), jnp.int32),
            jax.ShapeDtypeStruct((ROWS, D), BF16),
            jax.ShapeDtypeStruct((ROWS, 4 * D), F32),
        ),
        in_specs=[vmem_spec, vmem_spec, any_spec],
        out_specs=(any_spec,) * 5,
        scratch_shapes=[
            pltpu.VMEM((D, 4 * D), BF16),
            pltpu.VMEM((ROWS, D), BF16),
            pltpu.VMEM((ROWS, 4 * D), F32),
            pltpu.VMEM((ROWS, D), BF16),
            pltpu.VMEM((3, HEADS, 2, HALF, HEAD), BF16),
            pltpu.VMEM((1, 256), jnp.int32),
            dma((8,)), dma((2,)), dma((3, 8)), dma((3, 8)), dma((2, 8)), dma((2, 8)),
            dma((8,)), dma((8,)), dma((8,)), dma((8,)),
        ],
        compiler_params=pltpu.CompilerParams(
            collective_id=0, has_side_effects=True, vmem_limit_bytes=VMEM_LIMIT
        ),
        name="project_and_send",
    )(tokens, hist, w_in)


def column_of(row):
    wide = jnp.broadcast_to(row, (128, 128))
    on_diag = lax.broadcasted_iota(jnp.int32, (128, 128), 0) == lax.broadcasted_iota(
        jnp.int32, (128, 128), 1
    )
    return jnp.sum(jnp.where(on_diag, wide, 0), axis=1, keepdims=True)


def block_range(hist_s, first_block, last_block):
    first = hist_s[first_block, 0, 0]
    last = hist_s[last_block, 0, 128 + HALF - 1]
    low = jnp.int32(0)
    high = jnp.int32(CTX - 1)
    for c in range(CTX):
        low = low + (hist_s[c, 0, 128 + HALF - 1] < first).astype(jnp.int32)
        high = high - (hist_s[c, 0, 0] > last).astype(jnp.int32)
    return low, high


def lane_rows(hist_v, half, block, count):
    return [hist_v[block + n, :, half * 128 : half * 128 + HALF] for n in range(count)]


def attend_kernel(core_s, hist_s, hist_v, q_ref, kv_ref, out_ref, acc, row_f, hcol):
    core = core_s[0]
    for half in range(2):
        for group in range(4):
            row_f[half, group] = jnp.concatenate(lane_rows(hist_v, half, group * 4, 4), axis=1)

    def q_tile(tile, _):
        block_a = 4 * tile + core
        block_b = block_a + 2
        low, high = block_range(hist_s, block_a, block_b)
        for half in range(2):
            for n, block in enumerate((block_a, block_b)):
                col = column_of(hist_v[block, :, half * 128 : half * 128 + 128])
                hcol[n * HALF : (n + 1) * HALF] = col[:HALF]
            history = hcol[...]
            queries = jnp.concatenate([q_ref[2 * tile, half], q_ref[2 * tile + 1, half]], axis=0)
            acc[...] = jnp.zeros_like(acc)
            inner = lax.broadcasted_iota(jnp.int32, (ROWS, 1), 0)
            second = inner >= HALF
            q_block = jnp.where(second, block_b, block_a)
            q_in = jnp.where(second, inner - HALF, inner)
            q_pos = (31 - q_block if half else q_block) * HALF + q_in

            def step(group, k_half):
                keys = kv_ref[0, k_half, pl.ds(group * 4, 4)].reshape(4 * HALF, HEAD)
                values = kv_ref[1, k_half, pl.ds(group * 4, 4)].reshape(4 * HALF, HEAD)
                h = dot_nt(queries, keys) * (0.5 * SCALE)
                weights = h + h * jnp.tanh(h)
                visible = history == row_f[k_half, group]
                if half == k_half:
                    lane = lax.broadcasted_iota(jnp.int32, (1, 4 * HALF), 1)
                    inside = lane // HALF
                    k_block = group * 4 + inside
                    k_pos = (31 - k_block if half else k_block) * HALF + lane - inside * HALF
                    visible = visible & (k_pos <= q_pos)
                weights = jnp.where(visible, weights, 0.0).astype(BF16)
                acc[...] += dot_nn(weights, values)

            if half == 0:

                @pl.loop(low // 4, jnp.minimum(high, block_b) // 4 + 1)
                def _(group):
                    step(group, 0)
            else:

                @pl.loop(low // 4, high // 4 + 1)
                def _(group):
                    step(group, 0)

                @pl.loop(jnp.maximum(low, block_a) // 4, high // 4 + 1)
                def _(group):
                    step(group, 1)

            out_ref[2 * tile, half] = acc[0:HALF].astype(BF16)
            out_ref[2 * tile + 1, half] = acc[HALF:ROWS].astype(BF16)
        return 0

    lax.fori_loop(0, 4, q_tile, 0)


def attend(core, hist_all, q_got, kv_got):
    vmem_spec = pl.BlockSpec(memory_space=pltpu.VMEM)
    smem_spec = pl.BlockSpec(memory_space=pltpu.SMEM)
    return pl.pallas_call(
        attend_kernel,
        out_shape=jax.ShapeDtypeStruct((8, 2, HALF, HEAD), BF16),
        in_specs=[smem_spec, smem_spec, vmem_spec, vmem_spec, vmem_spec],
        out_specs=vmem_spec,
        scratch_shapes=[
            pltpu.VMEM((ROWS, HEAD), F32),
            pltpu.VMEM((2, 4, 1, 4 * HALF), jnp.int32),
            pltpu.VMEM((ROWS, 1), jnp.int32),
        ],
        compiler_params=pltpu.CompilerParams(vmem_limit_bytes=VMEM_LIMIT),
        name="attend",
    )(core, hist_all, hist_all, q_got, kv_got)


def middle_kernel(
    o_ref, tokens, u_act, grad_out, w_out, layer_out, do_got, gated_out, grad_u_out,
    mixed_got, send_buf, gate_buf, osend, orecv, gsend, grecv,
):
    place = Place()
    barrier = pltpu.get_barrier_semaphore()
    for n in range(8):
        signal_if_other(place, barrier, place.owner(n))
        signal_if_other(place, barrier, place.worker(n))
    self_work = (place.t % 2 == place.core) & (place.t // HEADS == place.core)
    pl.semaphore_wait(barrier, 16 - 2 * self_work.astype(jnp.int32))
    my_head = place.t % HEADS
    slot = place.t // 2

    def o_args(i):
        return (
            place.owner(i), o_ref.at[i], mixed_got.at[my_head], osend.at[i], orecv.at[my_head],
        )

    def g_args(head):
        return (
            place.worker(head), send_buf.at[head], do_got.at[slot], gsend.at[head], grecv.at[slot],
        )

    for i in range(8):
        start_copy(place, *o_args(i))
    grad_gated = dot_nt(grad_out[...], w_out[...])
    gate_buf[...] = grad_gated
    for head in range(HEADS):
        wait_arrived(mixed_got.at[head], orecv.at[head])
    mixed = jnp.concatenate(
        [mixed_got[head].reshape(ROWS, HEAD) for head in range(HEADS)], axis=1
    ).astype(F32)
    mixed_n, inv_o = norm_rows(mixed)
    gate_u = u_act[...].astype(F32)
    grad_gated = gate_buf[...]
    grad_mixed = norm_back(grad_gated * gate_u, mixed_n, inv_o).astype(BF16)
    for head in range(HEADS):
        send_buf[head] = grad_mixed[:, head * 128 : (head + 1) * 128].reshape(2, HALF, HEAD)
        start_copy(place, *g_args(head))
    grad_u_out[...] = grad_gated * mixed_n
    gated = (mixed_n * gate_u).astype(BF16)
    gated_out[...] = gated
    layer_out[...] = (dot_nn(gated, w_out[...]) + tokens[...].astype(F32)).astype(BF16)
    for i in range(8):
        wait_arrived(do_got.at[i], grecv.at[i])
    for n in range(8):
        wait_sent(place, *o_args(n))
        wait_sent(place, *g_args(n))


def middle(o_loc, tokens, u_act, grad_out, w_out):
    any_spec = pl.BlockSpec(memory_space=pl.ANY)
    vmem_spec = pl.BlockSpec(memory_space=pltpu.VMEM)
    dma = pltpu.SemaphoreType.DMA
    return pl.pallas_call(
        middle_kernel,
        out_shape=(
            jax.ShapeDtypeStruct((ROWS, D), BF16),
            jax.ShapeDtypeStruct((8, 2, HALF, HEAD), BF16),
            jax.ShapeDtypeStruct((ROWS, D), BF16),
            jax.ShapeDtypeStruct((ROWS, D), F32),
        ),
        in_specs=[vmem_spec] * 5,
        out_specs=(vmem_spec, any_spec, vmem_spec, vmem_spec),
        scratch_shapes=[
            pltpu.VMEM((HEADS, 2, HALF, HEAD), BF16),
            pltpu.VMEM((HEADS, 2, HALF, HEAD), BF16),
            pltpu.VMEM((ROWS, D), F32),
            dma((8,)), dma((8,)), dma((8,)), dma((8,)),
        ],
        compiler_params=pltpu.CompilerParams(
            collective_id=1, has_side_effects=True, vmem_limit_bytes=VMEM_LIMIT
        ),
        name="gate_and_send",
    )(o_loc, tokens, u_act, grad_out, w_out)


def attend_back_kernel(
    core_s, hist_s, hist_v, q_ref, kv_ref, do_ref, dq_ref, dkv_ref, dkv_acc, dq_acc, kcol, qrow
):
    core = core_s[0]
    dkv_acc[...] = jnp.zeros_like(dkv_acc)
    for half in range(2):
        for c in range(CTX):
            col = column_of(hist_v[c, :, half * 128 : half * 128 + 128])
            kcol[half, c // 2, (c % 2) * HALF : (c % 2 + 1) * HALF] = col[:HALF]

    def q_tile(tile, _):
        blocks = [8 * tile + 2 * n + core for n in range(4)]
        low, high = block_range(hist_s, blocks[0], blocks[3])
        for half in range(2):
            history = jnp.concatenate(
                [hist_v[block, :, half * 128 : half * 128 + HALF] for block in blocks], axis=1
            )
            qrow[...] = history
            queries = q_ref[pl.ds(4 * tile, 4), half].reshape(4 * HALF, HEAD)
            grads = do_ref[pl.ds(4 * tile, 4), half].reshape(4 * HALF, HEAD)
            dq_acc[...] = jnp.zeros_like(dq_acc)
            lane = lax.broadcasted_iota(jnp.int32, (1, 4 * HALF), 1)
            inside = lane // HALF
            q_block = blocks[0] + 2 * inside
            q_pos = (31 - q_block if half else q_block) * HALF + lane - inside * HALF

            def step(group, k_half):
                keys = kv_ref[0, k_half, pl.ds(group * 2, 2)].reshape(2 * HALF, HEAD)
                values = kv_ref[1, k_half, pl.ds(group * 2, 2)].reshape(2 * HALF, HEAD)
                h = dot_nt(keys, queries) * (0.5 * SCALE)
                grad_weights = dot_nt(values, grads)
                tanh_h = jnp.tanh(h)
                weights = h + h * tanh_h
                sigmoid_h = 0.5 + 0.5 * tanh_h
                slope = sigmoid_h + weights * (1.0 - sigmoid_h)
                visible = kcol[k_half, group] == qrow[...]
                if half == k_half:
                    inner = lax.broadcasted_iota(jnp.int32, (2 * HALF, 1), 0)
                    second = inner >= HALF
                    k_block = group * 2 + jnp.where(second, 1, 0)
                    k_in = jnp.where(second, inner - HALF, inner)
                    k_pos = (31 - k_block if half else k_block) * HALF + k_in
                    visible = visible & (k_pos <= q_pos)
                weights = jnp.where(visible, weights, 0.0).astype(BF16)
                grad_scores = jnp.where(visible, grad_weights * slope, 0.0).astype(BF16)
                dkv_acc[0, k_half, group] += dot_nn(grad_scores, queries)
                dkv_acc[1, k_half, group] += dot_nn(weights, grads)
                dq_acc[...] += dot_tn(grad_scores, keys)

            if half == 0:

                @pl.loop(low // 2, jnp.minimum(high, blocks[3]) // 2 + 1)
                def _(group):
                    step(group, 0)
            else:

                @pl.loop(low // 2, high // 2 + 1)
                def _(group):
                    step(group, 0)

                @pl.loop(jnp.maximum(low, blocks[0]) // 2, high // 2 + 1)
                def _(group):
                    step(group, 1)

            dq = (dq_acc[...] * SCALE).astype(BF16)
            for n in range(4):
                dq_ref[4 * tile + n, half] = dq[n * HALF : (n + 1) * HALF]
        return 0

    lax.fori_loop(0, 2, q_tile, 0)
    for parity in range(2):
        for half in range(2):
            rows = slice(parity * HALF, (parity + 1) * HALF)
            dkv_ref[parity, :, 0, half] = (dkv_acc[0, half, :, rows] * SCALE).astype(BF16)
            dkv_ref[parity, :, 1, half] = dkv_acc[1, half, :, rows].astype(BF16)


def attend_back(core, hist_all, q_got, kv_got, do_got):
    vmem_spec = pl.BlockSpec(memory_space=pltpu.VMEM)
    smem_spec = pl.BlockSpec(memory_space=pltpu.SMEM)
    return pl.pallas_call(
        attend_back_kernel,
        out_shape=(
            jax.ShapeDtypeStruct((8, 2, HALF, HEAD), BF16),
            jax.ShapeDtypeStruct((2, 8, 2, 2, HALF, HEAD), BF16),
        ),
        in_specs=[smem_spec, smem_spec, vmem_spec, vmem_spec, vmem_spec, vmem_spec],
        out_specs=(vmem_spec, vmem_spec),
        scratch_shapes=[
            pltpu.VMEM((2, 2, 8, ROWS, HEAD), F32),
            pltpu.VMEM((4 * HALF, HEAD), F32),
            pltpu.VMEM((2, 8, ROWS, 1), jnp.int32),
            pltpu.VMEM((1, 4 * HALF), jnp.int32),
        ],
        compiler_params=pltpu.CompilerParams(vmem_limit_bytes=VMEM_LIMIT),
        name="attend_back",
    )(core, hist_all, hist_all, q_got, kv_got, do_got)


def finish_kernel(
    dq_ref, dkv_ref, preact, w_in, grad_u, gated, tokens, grad_out, grad_tokens, out_grad,
    w_buf, pre_buf, sib_got, send_buf, got, rows_acc,
    g_send, g_got, g_sum, z_send, z_got, c_send, c_got,
    w_sem, p_sem, ssend, srecv, send_sem, recv_sem, gsend, grecv, zsend, zrecv, csend, crecv,
):
    place = Place()
    z = place.dp // 2
    my_head = place.t % HEADS

    p_copy = pltpu.make_async_copy(preact, pre_buf, p_sem)
    p_copy.start()

    def w_copy(n):
        cols = pl.ds(n * D, D)
        return pltpu.make_async_copy(w_in.at[:, cols], w_buf.at[:, cols], w_sem.at[n])

    for n in range(4):
        w_copy(n).start()

    barrier = pltpu.get_barrier_semaphore()
    for n in range(8):
        signal_if_other(place, barrier, place.worker(n))
    pl.semaphore_signal(barrier, inc=1, device_id=place.sibling)
    for n in range(1, 4):
        pl.semaphore_signal(
            barrier, inc=1, device_id={"dp": 2 * ((z + n) % 4) + place.core}
        )
    for n in range(1, CTX):
        pl.semaphore_signal(barrier, inc=1, device_id={"ctx": (place.t + n) % CTX})
    self_work = (place.t % 2 == place.core) & (place.t // HEADS == place.core)
    pl.semaphore_wait(barrier, 8 + 1 + 3 + 15 - self_work.astype(jnp.int32))

    to_sibling = pltpu.make_async_remote_copy(
        dkv_ref.at[1 - place.core], sib_got, ssend, srecv, device_id=place.sibling
    )
    to_sibling.start()

    def send_args(kind, i):
        src = dq_ref.at[i] if kind == 2 else send_buf.at[kind, i]
        return (
            place.owner(i), src, got.at[kind, my_head],
            send_sem.at[kind, i], recv_sem.at[kind, my_head],
        )

    for i in range(8):
        start_copy(place, *send_args(2, i))

    def product(chunk):
        cols = pl.ds(pl.multiple_of(chunk * 128, 128), 128)
        return dot_tn(grad_out[:, cols], gated[...])

    def to_core(n):
        return pltpu.make_async_remote_copy(
            g_send.at[n], g_got.at[n], gsend.at[n], grecv.at[n], device_id=place.sibling
        )

    for n in range(4):
        g_send[n] = product(2 * n + 1 - place.core).astype(BF16)
        to_core(n).start()

    to_sibling.wait_recv()
    for kind in range(2):
        for i in range(8):
            total = dkv_ref[place.core, i, kind].astype(F32) + sib_got[i, kind].astype(F32)
            send_buf[kind, i] = total.astype(BF16)
            start_copy(place, *send_args(kind, i))

    for n in range(4):
        g_sum[n] = product(2 * n + place.core)

    def to_plane(n):
        there = (z + n) % 4
        return pltpu.make_async_remote_copy(
            z_send.at[n - 1], z_got.at[n - 1], zsend.at[n - 1], zrecv.at[n - 1],
            device_id={"dp": 2 * there + place.core},
        )

    for n in range(4):
        to_core(n).wait_recv()
    for n in range(1, 4):
        there = (z + n) % 4
        z_send[n - 1] = (g_sum[there] + g_got[there].astype(F32)).astype(BF16)
        to_plane(n).start()

    p_copy.wait()
    w_copy(0).wait()

    def rows_part(gradient, col):
        cols = slice(col, col + D)
        _, slope = silu_and_grad(pre_buf[:, cols])
        return dot_nt((gradient * slope).astype(BF16), w_buf[:, cols])

    rows_acc[...] = rows_part(grad_u[...], U_COL)

    total = g_sum[z] + g_got[z].astype(F32)
    for n in range(1, 4):
        to_plane(n).wait_recv()
        total = total + z_got[n - 1].astype(F32)
    c_send[...] = total.reshape(CTX, 8, D)

    def to_ctx(n):
        there = (place.t + n) % CTX
        return pltpu.make_async_remote_copy(
            c_send.at[there], c_got.at[n - 1], csend.at[n - 1], crecv.at[n - 1],
            device_id={"ctx": there},
        )

    for n in range(1, CTX):
        to_ctx(n).start()

    for kind, col, w_index in ((2, Q_COL, 2), (0, K_COL, 3), (1, V_COL, 1)):
        w_copy(w_index).wait()
        for head in range(HEADS):
            wait_arrived(got.at[kind, head], recv_sem.at[kind, head])
        gradient = jnp.concatenate(
            [got[kind, head].reshape(ROWS, HEAD) for head in range(HEADS)], axis=1
        ).astype(F32)
        rows_acc[...] += rows_part(gradient, col)

    normed, inv_x = norm_rows(tokens[...].astype(F32))
    grad_tokens[...] = (
        grad_out[...].astype(F32) + norm_back(rows_acc[...], normed, inv_x)
    ).astype(BF16)

    total = c_send[place.t]
    for n in range(1, CTX):
        to_ctx(n).wait_recv()
        total = total + c_got[n - 1]
    out_grad[...] = total * (24576.0 ** (-0.5))

    to_sibling.wait_send()
    for n in range(4):
        to_core(n).wait_send()
    for n in range(1, 4):
        to_plane(n).wait_send()
    for n in range(1, CTX):
        to_ctx(n).wait_send()
    for i in range(8):
        for kind in range(3):
            wait_sent(place, *send_args(kind, i))


def finish(dq, dkv, preact, w_in, grad_u, gated, tokens, grad_out):
    any_spec = pl.BlockSpec(memory_space=pl.ANY)
    vmem_spec = pl.BlockSpec(memory_space=pltpu.VMEM)
    dma = pltpu.SemaphoreType.DMA
    return pl.pallas_call(
        finish_kernel,
        out_shape=(
            jax.ShapeDtypeStruct((ROWS, D), BF16),
            jax.ShapeDtypeStruct((8, D), F32),
        ),
        in_specs=[vmem_spec, vmem_spec, any_spec, any_spec] + [vmem_spec] * 4,
        out_specs=(vmem_spec, vmem_spec),
        scratch_shapes=[
            pltpu.VMEM((D, 4 * D), BF16),
            pltpu.VMEM((ROWS, 4 * D), F32),
            pltpu.VMEM((8, 2, 2, HALF, HEAD), BF16),
            pltpu.VMEM((2, 8, 2, HALF, HEAD), BF16),
            pltpu.VMEM((3, HEADS, 2, HALF, HEAD), BF16),
            pltpu.VMEM((ROWS, D), F32),
            pltpu.VMEM((4, 128, D), BF16),
            pltpu.VMEM((4, 128, D), BF16),
            pltpu.VMEM((4, 128, D), F32),
            pltpu.VMEM((3, 128, D), BF16),
            pltpu.VMEM((3, 128, D), BF16),
            pltpu.VMEM((CTX, 8, D), F32),
            pltpu.VMEM((CTX - 1, 8, D), F32),
            dma((4,)), dma, dma, dma, dma((3, 8)), dma((3, 8)),
            dma((4,)), dma((4,)), dma((3,)), dma((3,)), dma((CTX - 1,)), dma((CTX - 1,)),
        ],
        compiler_params=pltpu.CompilerParams(
            collective_id=2, has_side_effects=True, vmem_limit_bytes=VMEM_LIMIT
        ),
        name="return_and_finish",
    )(dq, dkv, preact, w_in, grad_u, gated, tokens, grad_out)


def on_device(tokens, segments, w_in, w_out, grad_out):
    core = (lax.axis_index("dp") % 2).astype(jnp.int32).reshape(1)
    q_got, kv_got, hist_all, u_act, preact = project(tokens, segments, w_in)
    o_loc = attend(core, hist_all, q_got, kv_got)
    layer_out, do_got, gated, grad_u = middle(o_loc, tokens, u_act, grad_out, w_out)
    dq, dkv = attend_back(core, hist_all, q_got, kv_got, do_got)
    grad_tokens, out_grad = finish(dq, dkv, preact, w_in, grad_u, gated, tokens, grad_out)
    return (layer_out, grad_tokens, out_grad)


def solution(mesh):
    return jax.shard_map(
        on_device,
        mesh=mesh,
        in_specs=(P(("dp", "ctx"), None), P("dp", "ctx"), P(), P(), P(("dp", "ctx"), None)),
        out_specs=(P(("dp", "ctx"), None), P(("dp", "ctx"), None), P(("dp", "ctx"), None)),
        check_vma=False,
    )
```

```python
import jax
import jax.numpy as jnp
from jax import lax
from jax.experimental import pallas as pl
from jax.experimental.pallas import tpu as pltpu
from jax.sharding import PartitionSpec as P

HEADS = 8
HEAD = 128
ROWS = 192
HALF = 96
D = 1024
CTX = 16
G = 4 * HALF
EPS = 1e-05
SCALE = HEAD ** (-0.5)
VMEM_LIMIT = 60 * 1024 * 1024
F32 = jnp.float32
BF16 = jnp.bfloat16
U_COL, V_COL, Q_COL, K_COL = 0, D, 2 * D, 3 * D
KEY, QUERY, VALUE, GNORM = 0, 1, 2, 3

TILES = [(0, 0, 0, 0), (0, 0, 0, 1)]
TILES += [(1, 0, 0, g) for g in range(4)] + [(1, 0, 1, g) for g in range(4)]
TILES += [(0, 1, 0, g) for g in range(4)]
TILES += [(1, 1, 0, g) for g in range(4)] + [(1, 1, 1, g) for g in (2, 3)]


def norm_rows(matrix):
    average = jnp.mean(matrix, axis=-1, keepdims=True)
    centred = matrix - average
    inverse = lax.rsqrt(jnp.mean(centred * centred, axis=-1, keepdims=True) + EPS)
    return centred * inverse, inverse


def norm_back(gradient, normed, inverse):
    first = jnp.mean(gradient, axis=-1, keepdims=True)
    second = jnp.mean(gradient * normed, axis=-1, keepdims=True)
    return (gradient - first - normed * second) * inverse


def dot_nt(left, right):
    return lax.dot_general(left, right, (((1,), (1,)), ((), ())), preferred_element_type=F32)


def dot_tn(left, right):
    return lax.dot_general(left, right, (((0,), (0,)), ((), ())), preferred_element_type=F32)


def dot_nn(left, right):
    return lax.dot_general(left, right, (((1,), (0,)), ((), ())), preferred_element_type=F32)


def flat(blocks):
    return blocks.reshape(-1, HEAD)


class Place:
    def __init__(self):
        self.dp = lax.axis_index("dp")
        self.t = lax.axis_index("ctx")
        self.plane = 2 * (self.dp // 2)
        self.core = self.dp % 2
        self.z = self.dp // 2
        self.sibling = {"dp": self.plane + 1 - self.core}
        self.head = self.t % HEADS
        self.slot = self.t // 2

    def worker(self, head):
        return self.plane + self.t % 2, self.core * HEADS + head

    def owner(self, i):
        return self.plane + self.t // HEADS, 2 * i + self.core

    def is_me(self, device):
        return (device[0] == self.dp) & (device[1] == self.t)

    def has_self(self):
        return (self.t % 2 == self.core) & (self.t // HEADS == self.core)


def ident(device):
    return {"dp": device[0], "ctx": device[1]}


def signal_if_other(place, barrier, device):
    @pl.when(jnp.logical_not(place.is_me(device)))
    def _():
        pl.semaphore_signal(barrier, inc=1, device_id=ident(device))


def start_copy(place, device, src, dst, send_sem, recv_sem):
    mine = place.is_me(device)

    @pl.when(mine)
    def _():
        pltpu.make_async_copy(src, dst, recv_sem).start()

    @pl.when(jnp.logical_not(mine))
    def _():
        pltpu.make_async_remote_copy(
            src, dst, send_sem, recv_sem, device_id=ident(device)
        ).start()


def wait_sent(place, device, src, dst, send_sem, recv_sem):
    @pl.when(jnp.logical_not(place.is_me(device)))
    def _():
        pltpu.make_async_remote_copy(
            src, dst, send_sem, recv_sem, device_id=ident(device)
        ).wait_send()


def wait_arrived(dst, recv_sem):
    pltpu.make_async_copy(dst, dst, recv_sem).wait()


def history_masks(hist_all, khist, qhist, core):
    for half in range(2):
        lanes = slice(half * 128, half * 128 + HALF)
        for g in range(4):
            row = jnp.concatenate([hist_all[4 * g + n, :, lanes] for n in range(4)], axis=1)
            rows = jnp.broadcast_to(row.astype(F32).astype(BF16), (16, G))
            khist[half, g] = dot_tn(rows, jnp.full((16, 128), 1.0 / 16, BF16))
        for g in range(2):
            row = jnp.concatenate(
                [hist_all[8 * g + 2 * n + core, :, lanes] for n in range(4)], axis=1
            )
            qhist[half, g] = row.astype(F32)


def query_positions(half, g, core):
    lane = lax.broadcasted_iota(jnp.int32, (1, G), 1)
    inside = lane // HALF
    block = 8 * g + 2 * inside + core
    return (31 - block if half else block) * HALF + lane - inside * HALF


def key_positions(half, g):
    row = lax.broadcasted_iota(jnp.int32, (G, 128), 0)
    inside = row // HALF
    block = 4 * g + inside
    return (31 - block if half else block) * HALF + row - inside * HALF


def three(matrix):
    return jnp.concatenate([matrix, matrix, matrix], axis=1)


def score_tile(n, q_got, k_got, khist, qhist, p_buf, s_buf, core):
    qh, qg, kh, kg = TILES[n]
    half = dot_nt(
        flat(k_got[kh, 4 * kg : 4 * kg + 4]), flat(q_got[qh, 4 * qg : 4 * qg + 4])
    ) * (0.5 * SCALE)
    up = 1.0 + jnp.tanh(half)
    weights = half * up
    slope = weights + (0.5 * up) * (1.0 - weights)
    visible = three(khist[kh, kg]) == qhist[qh, qg]
    if qh == kh and kg // 2 == qg:
        visible = visible & (three(key_positions(kh, kg)) <= query_positions(qh, qg, core))
    p_buf[n] = jnp.where(visible, weights, 0.0).astype(BF16)
    s_buf[n] = jnp.where(visible, slope, 0.0).astype(BF16)


def mix_tiles(qh, qg, vt, p_buf):
    total = None
    for n, tile in enumerate(TILES):
        if tile[:2] == (qh, qg):
            part = dot_nn(vt[tile[2], tile[3]], p_buf[n])
            total = part if total is None else total + part
    return total


def back_keys(kh, kg, q_got, v_got, kt, dot_buf, p_buf, s_buf, dqt):
    values = flat(v_got[kh, 4 * kg : 4 * kg + 4])
    grad_k = grad_v = None
    for n, tile in enumerate(TILES):
        if tile[2:] != (kh, kg):
            continue
        qh, qg = tile[:2]
        grads = dot_buf[qh, qg]
        grad_scores = (dot_nn(values, grads) * s_buf[n].astype(F32)).astype(BF16)
        part_v = dot_nt(p_buf[n], grads)
        part_k = dot_nn(grad_scores, flat(q_got[qh, 4 * qg : 4 * qg + 4]))
        grad_v = part_v if grad_v is None else grad_v + part_v
        grad_k = part_k if grad_k is None else grad_k + part_k
        dqt[qh, qg] += dot_nn(kt[kh, kg], grad_scores)
    return grad_k, grad_v


def layer_kernel(
    tokens_in, hist, w_in, w_out_in, grad_out_in,
    layer_out, grad_tokens, out_grad,
    tokens, grad_out, w_buf, w_out, normed_buf, slope_buf, u_buf, gate_buf,
    hist_buf, hist_all, khist, qhist,
    send_buf, k_got, v_got, q_got, n_got,
    p_buf, s_buf, vt, kt, ot_buf, gt_buf, o_send, mixed_got, stats, dot_buf, dqt,
    part, part_send, sib_got, ret_send, ret_got, rows_acc,
    go_sib, gated_buf, gated_sib, g_sum, z_send, z_got, c_send, c_got,
    in_sem, w_sem, hsend, hrecv, hfsend, hfrecv, send_sem, recv_sem, fsend, frecv,
    osend, orecv, ssend, srecv, psend, precv, rsend, rrecv,
    gosend, gorecv, gdsend, gdrecv, zsend, zrecv, csend, crecv,
):
    place = Place()
    core, t, z, my_head, slot = place.core, place.t, place.z, place.head, place.slot

    t_copy = pltpu.make_async_copy(tokens_in, tokens, in_sem.at[0])
    t_copy.start()
    chunks = [K_COL, K_COL + 512, Q_COL, Q_COL + 512, V_COL, V_COL + 512, U_COL, U_COL + 512]

    def w_copy(n):
        cols = pl.ds(chunks[n], 512)
        return pltpu.make_async_copy(w_in.at[:, cols], w_buf.at[:, cols], w_sem.at[n])

    for n in range(2):
        w_copy(n).start()
    go_copy = pltpu.make_async_copy(grad_out_in, grad_out, in_sem.at[1])
    go_copy.start()
    for n in range(2, 8):
        w_copy(n).start()
    wo_copy = pltpu.make_async_copy(w_out_in, w_out, in_sem.at[2])
    wo_copy.start()

    barrier = pltpu.get_barrier_semaphore()
    for n in range(8):
        signal_if_other(place, barrier, place.owner(n))
        signal_if_other(place, barrier, place.worker(n))
    pl.semaphore_signal(barrier, inc=1, device_id=place.sibling)
    for n in range(1, 4):
        pl.semaphore_signal(barrier, inc=1, device_id={"dp": 2 * ((z + n) % 4) + core})
    for n in range(1, CTX):
        pl.semaphore_signal(barrier, inc=1, device_id={"ctx": (t + n) % CTX})

    hist_buf[...] = jnp.zeros_like(hist_buf)
    hist_buf[:, 0:HALF] = hist[:, 0:HALF]
    hist_buf[:, 128 : 128 + HALF] = hist[:, HALF:ROWS]
    t_copy.wait()
    normed_buf[...] = norm_rows(tokens[...].astype(F32))[0].astype(BF16)

    def send_args(kind, head):
        got = (k_got, q_got, v_got, n_got)[kind]
        dst = got.at[:, t] if kind in (KEY, VALUE) else got.at[:, slot]
        return (
            place.worker(head), send_buf.at[kind, head], dst,
            send_sem.at[kind, head], recv_sem.at[kind, slot],
        )

    def hist_args(head):
        return place.worker(head), hist_buf, hist_all.at[t], hsend.at[head], hrecv.at[slot]

    def go_to_sibling(n):
        cols = pl.ds(pl.multiple_of((2 * n + 1 - core) * 128, 128), 128)
        return pltpu.make_async_remote_copy(
            grad_out.at[:, cols], go_sib.at[n], gosend.at[n], gorecv.at[n],
            device_id=place.sibling,
        )

    def project(n):
        w_copy(n).wait()
        cols = slice(chunks[n], chunks[n] + 512)
        half = 0.5 * dot_nn(normed_buf[...], w_buf[:, cols])
        up = 1.0 + jnp.tanh(half)
        act = half * up
        slope_buf[:, cols] = act + (0.5 * up) * (1.0 - act)
        return act.astype(BF16)

    for n in range(8):
        act = project(n)
        if n == 0:
            pl.semaphore_wait(barrier, 16 + 1 + 3 + 15 - 2 * place.has_self().astype(jnp.int32))
            for head in range(HEADS):
                start_copy(place, *hist_args(head))
        if n < 6:
            for j in range(4):
                head = (n % 2) * 4 + j
                send_buf[n // 2, head] = act[:, j * 128 : (j + 1) * 128].reshape(2, HALF, HEAD)
                start_copy(place, *send_args(n // 2, head))
        else:
            u_buf[:, chunks[n] : chunks[n] + 512] = act

    go_copy.wait()
    for n in range(4):
        go_to_sibling(n).start()
    wo_copy.wait()
    gate_buf[...] = dot_nt(grad_out[...], w_out[...])
    grad_norm = (gate_buf[...] * u_buf[...].astype(F32)).astype(BF16)
    for head in range(HEADS):
        send_buf[GNORM, head] = grad_norm[:, head * 128 : (head + 1) * 128].reshape(2, HALF, HEAD)
        start_copy(place, *send_args(GNORM, head))

    def hist_forward(i):
        c = 2 * i + core
        return pltpu.make_async_remote_copy(
            hist_all.at[c], hist_all.at[c], hfsend.at[i], hfrecv.at[i], device_id=place.sibling
        )

    def forward(kind, i):
        ref = (k_got, None, v_got)[kind].at[:, 2 * i + core]
        return pltpu.make_async_remote_copy(
            ref, ref, fsend.at[kind // 2, i], frecv.at[kind // 2, i], device_id=place.sibling
        )

    def pass_on(kind):
        got = (k_got, None, v_got)[kind]
        for i in range(8):
            wait_arrived(got.at[:, 2 * i + core], recv_sem.at[kind, i])
            forward(kind, i).start()

    def wait_passed(kind):
        got = (k_got, None, v_got)[kind]
        for i in range(8):
            wait_arrived(got.at[:, 2 * i + 1 - core], frecv.at[kind // 2, i])

    for i in range(8):
        wait_arrived(hist_all.at[2 * i + core], hrecv.at[i])
        hist_forward(i).start()
    for i in range(8):
        wait_arrived(hist_all.at[2 * i + 1 - core], hfrecv.at[i])
    history_masks(hist_all, khist, qhist, core)

    pass_on(KEY)
    for i in range(8):
        wait_arrived(q_got.at[:, i], recv_sem.at[QUERY, i])
    wait_passed(KEY)
    for n in range(12):
        score_tile(n, q_got, k_got, khist, qhist, p_buf, s_buf, core)
    pass_on(VALUE)
    for n in range(12, len(TILES)):
        score_tile(n, q_got, k_got, khist, qhist, p_buf, s_buf, core)
    wait_passed(VALUE)
    for half in range(2):
        for g in range(4):
            vt[half, g] = flat(v_got[half, 4 * g : 4 * g + 4]).T

    def o_args(i):
        return (
            place.owner(i), o_send.at[:, i], mixed_got.at[my_head], osend.at[i], orecv.at[my_head],
        )

    for qg in range(2):
        for qh in range(2):
            mixed_t = mix_tiles(qh, qg, vt, p_buf)
            ot_buf[qh, qg] = mixed_t
            o_send[qh, 4 * qg : 4 * qg + 4] = mixed_t.T.astype(BF16).reshape(4, HALF, HEAD)
            average = jnp.mean(mixed_t, axis=0, keepdims=True)
            centred = mixed_t - average
            stats[my_head, qg, 4 * qh : 4 * qh + 1] = average
            stats[my_head, qg, 4 * qh + 1 : 4 * qh + 2] = jnp.sum(
                centred * centred, axis=0, keepdims=True
            )
        for i in range(4 * qg, 4 * qg + 4):
            start_copy(place, *o_args(i))

    def stats_copy(n):
        there = (t // HEADS) * HEADS + (my_head + n) % HEADS
        return pltpu.make_async_remote_copy(
            stats.at[my_head], stats.at[my_head], ssend.at[n - 1], srecv.at[n - 1],
            device_id={"ctx": there},
        )

    for i in range(8):
        wait_arrived(n_got.at[:, i], recv_sem.at[GNORM, i])
    for qg in range(2):
        for qh in range(2):
            grad_t = flat(n_got[qh, 4 * qg : 4 * qg + 4]).T
            gt_buf[qh, qg] = grad_t
            grad_t = grad_t.astype(F32)
            average = stats[my_head, qg, 4 * qh : 4 * qh + 1]
            stats[my_head, qg, 4 * qh + 2 : 4 * qh + 3] = jnp.sum(grad_t, axis=0, keepdims=True)
            stats[my_head, qg, 4 * qh + 3 : 4 * qh + 4] = jnp.sum(
                grad_t * (ot_buf[qh, qg] - average), axis=0, keepdims=True
            )
    for n in range(1, HEADS):
        stats_copy(n).start()
    for half in range(2):
        for g in range(4):
            kt[half, g] = flat(k_got[half, 4 * g : 4 * g + 4]).T
    dqt[...] = jnp.zeros_like(dqt)
    for n in range(1, HEADS):
        wait_arrived(stats.at[(my_head + HEADS - n) % HEADS], srecv.at[n - 1])
    for qg in range(2):
        for qh in range(2):
            rows = [[stats[h, qg, 4 * qh + k : 4 * qh + k + 1] for h in range(HEADS)] for k in range(4)]
            average = sum(rows[0]) * (1.0 / HEADS)
            off = [row - average for row in rows[0]]
            spread = sum(rows[1]) + HEAD * sum(o * o for o in off)
            inverse = lax.rsqrt(spread * (1.0 / D) + EPS)
            first = sum(rows[2]) * (1.0 / D)
            second = (sum(rows[3]) + sum(o * a for o, a in zip(off, rows[2]))) * (1.0 / D)
            centred = ot_buf[qh, qg] - average
            dot_buf[qh, qg] = (
                (gt_buf[qh, qg].astype(F32) - first - centred * (second * inverse * inverse))
                * inverse
            ).astype(BF16)

    def gate():
        for head in range(HEADS):
            wait_arrived(mixed_got.at[head], orecv.at[head])
        mixed = jnp.concatenate([flat(mixed_got[head]) for head in range(HEADS)], axis=1)
        mixed_n, _ = norm_rows(mixed.astype(F32))
        gated = (mixed_n * u_buf[...].astype(F32)).astype(BF16)
        gated_buf[...] = gated
        gated_copy.start()
        grad_pre = (gate_buf[...] * mixed_n * slope_buf[:, U_COL : U_COL + D]).astype(BF16)
        layer_out[...] = (dot_nn(gated, w_out[...]) + tokens[...].astype(F32)).astype(BF16)
        rows_acc[...] = dot_nt(grad_pre, w_buf[:, U_COL : U_COL + D])

    gated_copy = pltpu.make_async_remote_copy(
        gated_buf, gated_sib, gdsend, gdrecv, device_id=place.sibling
    )

    def to_plane(n):
        return pltpu.make_async_remote_copy(
            z_send.at[n - 1], z_got.at[n - 1], zsend.at[n - 1], zrecv.at[n - 1],
            device_id={"dp": 2 * ((z + n) % 4) + core},
        )

    def products():
        gated_copy.wait_recv()
        for n in range(4):
            go_to_sibling(n).wait_recv()
        for n in (2, 1, 3, 0):
            there = (z + n) % 4
            cols = pl.ds(pl.multiple_of((2 * there + core) * 128, 128), 128)
            product = dot_tn(grad_out[:, cols], gated_buf[...]) + dot_tn(
                go_sib[there], gated_sib[...]
            )
            if n:
                z_send[n - 1] = product.astype(BF16)
                to_plane(n).start()
            else:
                g_sum[...] = product

    def part_copy(kind, kg, kh):
        ref = part_send.at[kind, kg, kh]
        return pltpu.make_async_remote_copy(
            ref, sib_got.at[kind, kg, kh], psend.at[kind, kg, kh], precv.at[kind, kg, kh],
            device_id=place.sibling,
        )

    def ret_args(kind, i):
        return (
            place.owner(i), ret_send.at[kind, i], ret_got.at[kind, my_head],
            rsend.at[kind, i], rrecv.at[kind, my_head],
        )

    def back_group(kg):
        for kh in range(2):
            grads = back_keys(kh, kg, q_got, v_got, kt, dot_buf, p_buf, s_buf, dqt)
            for kind in range(2):
                grad = grads[kind] * SCALE if kind == 0 else grads[kind]
                grad = grad.reshape(2, 2, HALF, HEAD)
                for parity in range(2):
                    part[kind, kg, kh, parity] = grad[:, parity]
                part_send[kind, kg, kh] = part[kind, kg, kh, 1 - core].astype(BF16)
                part_copy(kind, kg, kh).start()

    def return_group(kg):
        for kind in (1, 0):
            for kh in range(2):
                part_copy(kind, kg, kh).wait_recv()
                total = part[kind, kg, kh, core] + sib_got[kind, kg, kh].astype(F32)
                for n in range(2):
                    ret_send[kind, 2 * kg + n, kh] = total[n].astype(BF16)
            for n in range(2):
                start_copy(place, *ret_args(kind, 2 * kg + n))

    back_group(0)
    gate()
    back_group(1)
    return_group(0)
    products()
    back_group(2)
    return_group(1)
    back_group(3)
    return_group(2)
    for qg in range(2):
        for qh in range(2):
            grad_q = (dqt[qh, qg] * SCALE).T.astype(BF16).reshape(4, HALF, HEAD)
            for n in range(4):
                ret_send[2, 4 * qg + n, qh] = grad_q[n]
        if qg == 0:
            return_group(3)
        for i in range(4 * qg, 4 * qg + 4):
            start_copy(place, *ret_args(2, i))

    total = g_sum[...]
    for n in range(1, 4):
        to_plane(n).wait_recv()
        total = total + z_got[n - 1].astype(F32)
    c_send[...] = total.reshape(CTX, 8, D)

    def to_ctx(n):
        there = (t + n) % CTX
        return pltpu.make_async_remote_copy(
            c_send.at[there], c_got.at[n - 1], csend.at[n - 1], crecv.at[n - 1],
            device_id={"ctx": there},
        )

    for n in range(1, CTX):
        to_ctx(n).start()

    for kind, col in ((1, V_COL), (0, K_COL), (2, Q_COL)):
        for head in range(HEADS):
            wait_arrived(ret_got.at[kind, head], rrecv.at[kind, head])
        gradient = jnp.concatenate([flat(ret_got[kind, head]) for head in range(HEADS)], axis=1)
        grad_pre = (gradient.astype(F32) * slope_buf[:, col : col + D]).astype(BF16)
        rows_acc[...] += dot_nt(grad_pre, w_buf[:, col : col + D])

    normed, inv_x = norm_rows(tokens[...].astype(F32))
    grad_tokens[...] = (
        grad_out[...].astype(F32) + norm_back(rows_acc[...], normed, inv_x)
    ).astype(BF16)

    total = c_send[t]
    for n in range(1, CTX):
        to_ctx(n).wait_recv()
        total = total + c_got[n - 1]
    out_grad[...] = total * (24576.0 ** (-0.5))

    for n in range(4):
        go_to_sibling(n).wait_send()
    gated_copy.wait_send()
    for n in range(1, 4):
        to_plane(n).wait_send()
    for n in range(1, CTX):
        to_ctx(n).wait_send()
    for n in range(1, HEADS):
        stats_copy(n).wait_send()
    for i in range(8):
        hist_forward(i).wait_send()
        forward(KEY, i).wait_send()
        forward(VALUE, i).wait_send()
        wait_sent(place, *hist_args(i))
        for kind in range(4):
            wait_sent(place, *send_args(kind, i))
        wait_sent(place, *o_args(i))
        for kind in range(3):
            wait_sent(place, *ret_args(kind, i))
    for kind in range(2):
        for kg in range(4):
            for kh in range(2):
                part_copy(kind, kg, kh).wait_send()


def on_device(tokens, segments, w_in, w_out, grad_out):
    any_spec = pl.BlockSpec(memory_space=pl.ANY)
    vmem_spec = pl.BlockSpec(memory_space=pltpu.VMEM)
    dma = pltpu.SemaphoreType.DMA
    vmem = pltpu.VMEM
    tiles = len(TILES)
    return pl.pallas_call(
        layer_kernel,
        out_shape=(
            jax.ShapeDtypeStruct((ROWS, D), BF16),
            jax.ShapeDtypeStruct((ROWS, D), BF16),
            jax.ShapeDtypeStruct((8, D), F32),
        ),
        in_specs=[any_spec, vmem_spec, any_spec, any_spec, any_spec],
        out_specs=(vmem_spec, vmem_spec, vmem_spec),
        scratch_shapes=[
            vmem((ROWS, D), BF16),
            vmem((ROWS, D), BF16),
            vmem((D, 4 * D), BF16),
            vmem((D, D), BF16),
            vmem((ROWS, D), BF16),
            vmem((ROWS, 4 * D), F32),
            vmem((ROWS, D), BF16),
            vmem((ROWS, D), F32),
            vmem((1, 256), jnp.int32),
            vmem((CTX, 1, 256), jnp.int32),
            vmem((2, 4, G, 128), F32),
            vmem((2, 2, 1, G), F32),
            vmem((4, HEADS, 2, HALF, HEAD), BF16),
            vmem((2, CTX, HALF, HEAD), BF16),
            vmem((2, CTX, HALF, HEAD), BF16),
            vmem((2, 8, HALF, HEAD), BF16),
            vmem((2, 8, HALF, HEAD), BF16),
            vmem((tiles, G, G), BF16),
            vmem((tiles, G, G), BF16),
            vmem((2, 4, HEAD, G), BF16),
            vmem((2, 4, HEAD, G), BF16),
            vmem((2, 2, HEAD, G), F32),
            vmem((2, 2, HEAD, G), BF16),
            vmem((2, 8, HALF, HEAD), BF16),
            vmem((HEADS, 2, HALF, HEAD), BF16),
            vmem((HEADS, 2, 8, G), F32),
            vmem((2, 2, HEAD, G), BF16),
            vmem((2, 2, HEAD, G), F32),
            vmem((2, 4, 2, 2, 2, HALF, HEAD), F32),
            vmem((2, 4, 2, 2, HALF, HEAD), BF16),
            vmem((2, 4, 2, 2, HALF, HEAD), BF16),
            vmem((3, 8, 2, HALF, HEAD), BF16),
            vmem((3, HEADS, 2, HALF, HEAD), BF16),
            vmem((ROWS, D), F32),
            vmem((4, ROWS, 128), BF16),
            vmem((ROWS, D), BF16),
            vmem((ROWS, D), BF16),
            vmem((128, D), F32),
            vmem((3, 128, D), BF16),
            vmem((3, 128, D), BF16),
            vmem((CTX, 8, D), F32),
            vmem((CTX - 1, 8, D), F32),
            dma((3,)), dma((8,)),
            dma((8,)), dma((8,)), dma((8,)), dma((8,)),
            dma((4, 8)), dma((4, 8)), dma((2, 8)), dma((2, 8)),
            dma((8,)), dma((8,)), dma((HEADS - 1,)), dma((HEADS - 1,)),
            dma((2, 4, 2)), dma((2, 4, 2)), dma((3, 8)), dma((3, 8)),
            dma((4,)), dma((4,)), dma, dma,
            dma((3,)), dma((3,)), dma((CTX - 1,)), dma((CTX - 1,)),
        ],
        compiler_params=pltpu.CompilerParams(
            collective_id=0, has_side_effects=True, vmem_limit_bytes=VMEM_LIMIT
        ),
        name="layer",
    )(tokens, segments, w_in, w_out, grad_out)


def solution(mesh):
    return jax.shard_map(
        on_device,
        mesh=mesh,
        in_specs=(P(("dp", "ctx"), None), P("dp", "ctx"), P(), P(), P(("dp", "ctx"), None)),
        out_specs=(P(("dp", "ctx"), None), P(("dp", "ctx"), None), P(("dp", "ctx"), None)),
        check_vma=False,
    )
```

```python
import jax
import jax.numpy as jnp
from jax import lax
from jax.experimental import pallas as pl
from jax.experimental.pallas import tpu as pltpu
from jax.sharding import PartitionSpec as P

HEADS = 8
HEAD = 128
ROWS = 192
HALF = 96
D = 1024
CTX = 16
G = 4 * HALF
EPS = 1e-05
SCALE = HEAD ** (-0.5)
VMEM_LIMIT = 60 * 1024 * 1024
F32 = jnp.float32
BF16 = jnp.bfloat16
U_COL, V_COL, Q_COL, K_COL = 0, D, 2 * D, 3 * D
KEY, QUERY, VALUE, GNORM = 0, 1, 2, 3

TILES = [(0, 0, 0, 0), (0, 0, 0, 1)]
TILES += [(1, 0, 0, g) for g in range(4)] + [(1, 0, 1, g) for g in range(4)]
TILES += [(0, 1, 0, g) for g in range(4)]
TILES += [(1, 1, 0, g) for g in range(4)] + [(1, 1, 1, g) for g in (2, 3)]
FIRST = {(0, 0, 0): 0, (1, 0, 0): 2, (1, 0, 1): 6, (0, 1, 0): 10, (1, 1, 0): 14, (1, 1, 1): 16}


def norm_rows(matrix):
    average = jnp.mean(matrix, axis=-1, keepdims=True)
    centred = matrix - average
    inverse = lax.rsqrt(jnp.mean(centred * centred, axis=-1, keepdims=True) + EPS)
    return centred * inverse, inverse


def norm_back(gradient, normed, inverse):
    first = jnp.mean(gradient, axis=-1, keepdims=True)
    second = jnp.mean(gradient * normed, axis=-1, keepdims=True)
    return (gradient - first - normed * second) * inverse


def dot_nt(left, right):
    return lax.dot_general(left, right, (((1,), (1,)), ((), ())), preferred_element_type=F32)


def dot_tn(left, right):
    return lax.dot_general(left, right, (((0,), (0,)), ((), ())), preferred_element_type=F32)


def dot_nn(left, right):
    return lax.dot_general(left, right, (((1,), (0,)), ((), ())), preferred_element_type=F32)


def flat(blocks):
    return blocks.reshape(-1, HEAD)


class Place:
    def __init__(self):
        self.dp = lax.axis_index("dp")
        self.t = lax.axis_index("ctx")
        self.plane = 2 * (self.dp // 2)
        self.core = self.dp % 2
        self.z = self.dp // 2
        self.sibling = {"dp": self.plane + 1 - self.core}
        self.head = self.t % HEADS
        self.slot = self.t // 2

    def worker(self, head):
        return self.plane + self.t % 2, self.core * HEADS + head

    def owner(self, i):
        return self.plane + self.t // HEADS, 2 * i + self.core

    def is_me(self, device):
        return (device[0] == self.dp) & (device[1] == self.t)

    def has_self(self):
        return (self.t % 2 == self.core) & (self.t // HEADS == self.core)


def ident(device):
    return {"dp": device[0], "ctx": device[1]}


def signal_if_other(place, barrier, device):
    @pl.when(jnp.logical_not(place.is_me(device)))
    def _():
        pl.semaphore_signal(barrier, inc=1, device_id=ident(device))


def start_copy(place, device, src, dst, send_sem, recv_sem):
    mine = place.is_me(device)

    @pl.when(mine)
    def _():
        pltpu.make_async_copy(src, dst, recv_sem).start()

    @pl.when(jnp.logical_not(mine))
    def _():
        pltpu.make_async_remote_copy(
            src, dst, send_sem, recv_sem, device_id=ident(device)
        ).start()


def wait_sent(place, ref, sem):
    pltpu.make_async_remote_copy(ref, ref, sem, sem, device_id=place.sibling).wait_send()


def wait_sent_eight(place, ref, sem):
    @pl.when(place.has_self())
    def _():
        wait_sent(place, ref.at[0:7], sem)

    @pl.when(jnp.logical_not(place.has_self()))
    def _():
        wait_sent(place, ref, sem)


def wait_arrived(dst, recv_sem):
    pltpu.make_async_copy(dst, dst, recv_sem).wait()


def history_masks(hist_all, khist, qhist, core):
    for half in range(2):
        lanes = slice(half * 128, half * 128 + HALF)
        for g in range(4):
            row = jnp.concatenate(
                [hist_all[n // 2, 2 * g + n % 2, :, lanes] for n in range(4)], axis=1
            )
            rows = jnp.broadcast_to(row.astype(F32).astype(BF16), (16, G))
            khist[half, g] = dot_tn(rows, jnp.full((16, 128), 1.0 / 16, BF16))
        for g in range(2):
            row = jnp.concatenate(
                [hist_all[core, 4 * g + n, :, lanes] for n in range(4)], axis=1
            )
            qhist[half, g] = row.astype(F32)


def query_positions(half, g, core):
    lane = lax.broadcasted_iota(jnp.int32, (1, G), 1)
    inside = lane // HALF
    block = 8 * g + 2 * inside + core
    return (31 - block if half else block) * HALF + lane - inside * HALF


def key_positions(half, g):
    row = lax.broadcasted_iota(jnp.int32, (G, 128), 0)
    inside = row // HALF
    block = 4 * g + 2 * (inside % 2) + inside // 2
    return (31 - block if half else block) * HALF + row - inside * HALF


def key_rows(got, half, g):
    return jnp.concatenate([flat(got[half, n, pl.ds(2 * g, 2)]) for n in range(2)], axis=0)


def three(matrix):
    return jnp.concatenate([matrix, matrix, matrix], axis=1)


def score_tile(n, q_got, k_got, khist, qhist, p_buf, s_buf, core):
    qh, qg, kh, kg = TILES[n]
    half = dot_nt(
        key_rows(k_got, kh, kg), flat(q_got[qh, 4 * qg : 4 * qg + 4])
    ) * (0.5 * SCALE)
    up = 1.0 + jnp.tanh(half)
    weights = half * up
    slope = weights + (0.5 * up) * (1.0 - weights)
    visible = three(khist[kh, kg]) == qhist[qh, qg]
    if qh == kh and kg // 2 == qg:
        visible = visible & (three(key_positions(kh, kg)) <= query_positions(qh, qg, core))
    p_buf[n] = jnp.where(visible, weights, 0.0).astype(BF16)
    s_buf[n] = jnp.where(visible, slope, 0.0).astype(BF16)


def mix_tiles(qh, qg, vt, p_buf):
    total = None
    for n, tile in enumerate(TILES):
        if tile[:2] == (qh, qg):
            part = dot_nn(vt[tile[2], tile[3]], p_buf[n])
            total = part if total is None else total + part
    return total


def back_tile(tile, n, q_got, v_got, kt, dot_buf, p_buf, s_buf, dqt):
    qh, qg, kh, kg = tile
    grads = dot_buf[qh, qg]
    grad_scores = dot_nn(key_rows(v_got, kh, kg), grads) * s_buf[n].astype(F32)
    grad_scores = grad_scores.astype(BF16)
    grad_v = dot_nt(p_buf[n], grads)
    grad_k = dot_nn(grad_scores, flat(q_got[qh, 4 * qg : 4 * qg + 4]))
    dqt[qh, qg] += dot_nn(kt[kh, kg], grad_scores)
    return grad_k, grad_v


def layer_kernel(
    tokens_in, hist, w_in, w_out_in, grad_out_in,
    layer_out, grad_tokens, out_grad,
    tokens, go_all, w_buf, w_out, normed_buf, slope_buf, u_buf, gate_buf,
    hist_buf, hist_all, khist, qhist,
    send_buf, k_got, v_got, q_got, n_got,
    p_buf, s_buf, vt, kt, ot_buf, gt_buf, o_send, mixed_got, mean_send, mean_got, stats, dot_buf, dqt,
    low_buf, grads_buf, part, part_send, sib_got, ret_send, ret_got, rows_acc,
    gated_buf, gpre_buf, gd_got, g_buf, c_send, c_got, f_send, f_got,
    in_sem, w_sem, hsend, hrecv, hfsend, hfrecv, send_sem, recv_sem, fsend, frecv,
    osend, orecv, msend, mrecv, ssend, srecv, psend, precv, rsend, rrecv,
    zsend, zrecv, gfsend, gfrecv, gdsend, gdrecv, csend, crecv, fin_send, fin_recv,
):
    place = Place()
    core, t, z, my_head, slot, dp = place.core, place.t, place.z, place.head, place.slot, place.dp

    t_copy = pltpu.make_async_copy(tokens_in, tokens, in_sem.at[0])
    t_copy.start()
    chunks = [K_COL, K_COL + 512, Q_COL, Q_COL + 512, V_COL, V_COL + 512, U_COL, U_COL + 512]

    def w_copy(n):
        cols = pl.ds(chunks[n], 512)
        return pltpu.make_async_copy(w_in.at[:, cols], w_buf.at[:, cols], w_sem.at[n])

    for n in range(2):
        w_copy(n).start()
    go_copy = pltpu.make_async_copy(grad_out_in, go_all.at[dp], in_sem.at[1])
    go_copy.start()
    for n in range(2, 8):
        w_copy(n).start()
    wo_copy = pltpu.make_async_copy(w_out_in, w_out, in_sem.at[2])
    wo_copy.start()

    barrier = pltpu.get_barrier_semaphore()
    for n in range(8):
        signal_if_other(place, barrier, place.owner(n))
        signal_if_other(place, barrier, place.worker(n))
    for n in range(1, 8):
        pl.semaphore_signal(barrier, inc=1, device_id={"dp": (dp + n) % 8})
    for n in range(1, CTX):
        pl.semaphore_signal(barrier, inc=1, device_id={"ctx": (t + n) % CTX})

    hist_buf[...] = jnp.zeros_like(hist_buf)
    hist_buf[:, 0:HALF] = hist[:, 0:HALF]
    hist_buf[:, 128 : 128 + HALF] = hist[:, HALF:ROWS]
    t_copy.wait()
    normed_buf[...] = norm_rows(tokens[...].astype(F32))[0].astype(BF16)

    def send_args(kind, head, half):
        got = (k_got, q_got, v_got, n_got)[kind]
        dst = got.at[half, t % 2, slot] if kind in (KEY, VALUE) else got.at[half, slot]
        batch = slot // 4 if kind in (KEY, VALUE) else 0
        return (
            place.worker(head), send_buf.at[kind, half, head], dst,
            send_sem.at[kind, half], recv_sem.at[kind, half, batch],
        )

    def hist_args(head):
        return place.worker(head), hist_buf, hist_all.at[t % 2, slot], hsend, hrecv

    def go_along(n):
        ref = go_all.at[dp]
        return pltpu.make_async_remote_copy(
            ref, ref, zsend.at[n - 1], zrecv.at[n - 1], device_id={"dp": (dp + 2 * n) % 8}
        )

    def go_across(n):
        ref = go_all.at[(dp + 8 - 2 * n) % 8]
        return pltpu.make_async_remote_copy(
            ref, ref, gfsend.at[n], gfrecv.at[n], device_id=place.sibling
        )

    def project(n):
        w_copy(n).wait()
        cols = slice(chunks[n], chunks[n] + 512)
        half = 0.5 * dot_nn(normed_buf[...], w_buf[:, cols])
        up = 1.0 + jnp.tanh(half)
        act = half * up
        slope_buf[:, cols] = act + (0.5 * up) * (1.0 - act)
        return act.astype(BF16)

    for n in range(8):
        act = project(n)
        if n == 0:
            pl.semaphore_wait(barrier, 16 + 7 + 15 - 2 * place.has_self().astype(jnp.int32))
            for head in range(HEADS):
                start_copy(place, *hist_args(head))
        if n < 6:
            for j in range(4):
                head = (n % 2) * 4 + j
                for half in range(2):
                    send_buf[n // 2, half, head] = act[
                        half * HALF : (half + 1) * HALF, j * 128 : (j + 1) * 128
                    ]
                start_copy(place, *send_args(n // 2, head, 0))
        else:
            u_buf[:, chunks[n] : chunks[n] + 512] = act

    go_copy.wait()
    wo_copy.wait()
    gate_buf[...] = dot_nt(go_all[dp], w_out[...])
    grad_norm = (gate_buf[...] * u_buf[...].astype(F32)).astype(BF16)
    for head in range(HEADS):
        for half in range(2):
            send_buf[GNORM, half, head] = grad_norm[
                half * HALF : (half + 1) * HALF, head * 128 : (head + 1) * 128
            ]
        start_copy(place, *send_args(GNORM, head, 0))
    for kind in (QUERY, KEY, VALUE, GNORM):
        for head in range(HEADS):
            start_copy(place, *send_args(kind, head, 1))
    for n in (2, 1, 3):
        go_along(n).start()
    go_across(0).start()

    def hist_forward():
        ref = hist_all.at[core]
        return pltpu.make_async_remote_copy(ref, ref, hfsend, hfrecv, device_id=place.sibling)

    def forward(kind, half, batch):
        ref = (k_got, None, v_got)[kind].at[half, core, 4 * batch : 4 * batch + 4]
        return pltpu.make_async_remote_copy(
            ref, ref, fsend.at[kind // 2, half, batch], frecv.at[kind // 2, half, batch],
            device_id=place.sibling,
        )

    def pass_on(kind, half):
        got = (k_got, None, v_got)[kind]
        for batch in range(2):
            wait_arrived(
                got.at[half, core, 4 * batch : 4 * batch + 4], recv_sem.at[kind, half, batch]
            )
            forward(kind, half, batch).start()

    def wait_passed(kind, half):
        for batch in range(2):
            forward(kind, half, batch).wait_recv()

    def wait_rows(kind, half):
        got = (None, q_got, None, n_got)[kind]
        wait_arrived(got.at[half], recv_sem.at[kind, half, 0])

    wait_arrived(hist_all.at[core], hrecv)
    hist_forward().start()
    hist_forward().wait_recv()
    history_masks(hist_all, khist, qhist, core)

    def scores(qh, kh):
        for n, tile in enumerate(TILES):
            if (tile[0], tile[2]) == (qh, kh):
                score_tile(n, q_got, k_got, khist, qhist, p_buf, s_buf, core)

    def mean_args(i):
        return place.owner(i), mean_send.at[i], mean_got.at[my_head], msend, mrecv

    def o_args(i, half):
        return (
            place.owner(i), o_send.at[half, i], mixed_got.at[half, my_head],
            osend.at[half], orecv.at[half],
        )

    def mix(qh):
        for g in range(4):
            vt[qh, g] = key_rows(v_got, qh, g).T
        for qg in range(2):
            mixed_t = mix_tiles(qh, qg, vt, p_buf)
            average = jnp.mean(mixed_t, axis=0, keepdims=True)
            centred = mixed_t - average
            ot_buf[qh, qg] = centred
            o_send[qh, 4 * qg : 4 * qg + 4] = centred.T.astype(BF16).reshape(4, HALF, HEAD)
            for n in range(4):
                mean_send[4 * qg + n, :, qh * 128 : qh * 128 + HALF] = average[
                    :, n * HALF : (n + 1) * HALF
                ]
            stats[my_head, qh, 4 * qg : 4 * qg + 1] = average
            stats[my_head, qh, 4 * qg + 1 : 4 * qg + 2] = jnp.sum(
                centred * centred, axis=0, keepdims=True
            )

    def stats_copy(qh, n):
        there = (t // HEADS) * HEADS + (my_head + n) % HEADS
        ref = stats.at[my_head, qh]
        return pltpu.make_async_remote_copy(
            ref, ref, ssend.at[qh], srecv.at[qh], device_id={"ctx": there}
        )

    def send_stats(qh):
        wait_rows(GNORM, qh)
        for qg in range(2):
            grad_t = flat(n_got[qh, 4 * qg : 4 * qg + 4]).T
            gt_buf[qh, qg] = grad_t
            grad_t = grad_t.astype(F32)
            stats[my_head, qh, 4 * qg + 2 : 4 * qg + 3] = jnp.sum(grad_t, axis=0, keepdims=True)
            stats[my_head, qh, 4 * qg + 3 : 4 * qg + 4] = jnp.sum(
                grad_t * ot_buf[qh, qg], axis=0, keepdims=True
            )
        for n in range(1, HEADS):
            stats_copy(qh, n).start()

    def grads_of_mixed(qh):
        wait_arrived(stats.at[0:7, qh], srecv.at[qh])
        for qg in range(2):
            rows = [
                [stats[h, qh, 4 * qg + k : 4 * qg + k + 1] for h in range(HEADS)] for k in range(4)
            ]
            average = sum(rows[0]) * (1.0 / HEADS)
            off = [row - average for row in rows[0]]
            spread = sum(rows[1]) + HEAD * sum(o * o for o in off)
            inverse = lax.rsqrt(spread * (1.0 / D) + EPS)
            first = sum(rows[2]) * (1.0 / D)
            second = (sum(rows[3]) + sum(o * a for o, a in zip(off, rows[2]))) * (1.0 / D)
            centred = ot_buf[qh, qg] + (stats[my_head, qh, 4 * qg : 4 * qg + 1] - average)
            dot_buf[qh, qg] = (
                (gt_buf[qh, qg].astype(F32) - first - centred * (second * inverse * inverse))
                * inverse
            ).astype(BF16)

    def turn_keys(half):
        for g in range(4):
            kt[half, g] = key_rows(k_got, half, g).T

    def part_copy(kind, kg, kh):
        ref = part_send.at[kind, kg, kh]
        return pltpu.make_async_remote_copy(
            ref, sib_got.at[kind, kg, kh], psend.at[kind, kg, kh], precv.at[kind, kg, kh],
            device_id=place.sibling,
        )

    def ret_args(kind, i, half):
        return (
            place.owner(i), ret_send.at[kind, half, i], ret_got.at[kind, half, my_head],
            rsend.at[kind, half], rrecv.at[kind, half],
        )

    def back(qh, qg, kh, kg):
        n = FIRST[qh, qg, kh] + kg
        return back_tile(
            (qh, qg, kh, kg), n, q_got, v_got, kt, dot_buf, p_buf, s_buf, dqt
        )

    def back_lower():
        for kg in range(4):
            grad_k, grad_v = back(0, 1, 0, kg)
            if kg < 2:
                term_k, term_v = back(0, 0, 0, kg)
                grad_k, grad_v = grad_k + term_k, grad_v + term_v
            low_buf[0, kg], low_buf[1, kg] = grad_k, grad_v

    def group_at(step):
        return (step + t) % 4

    def back_part(step, kh):
        kg = group_at(step)
        grad_k, grad_v = back(1, 0, kh, kg)
        if kh == 0:
            term_k, term_v = back(1, 1, kh, kg)
            grads_buf[0] = (grad_k + term_k) + low_buf[0, kg]
            grads_buf[1] = (grad_v + term_v) + low_buf[1, kg]
        else:
            grads_buf[0], grads_buf[1] = grad_k, grad_v

            @pl.when(kg >= 2)
            def _():
                term_k, term_v = back(1, 1, kh, kg)
                grads_buf[0] += term_k
                grads_buf[1] += term_v

        for kind in (1, 0):
            grad = grads_buf[kind] * SCALE if kind == 0 else grads_buf[kind]
            grad = grad.reshape(2, 2, HALF, HEAD)
            for parity in range(2):
                part[kind, step, kh, parity] = grad[parity]
            part_send[kind, step, kh] = part[kind, step, kh, 1 - core].astype(BF16)
            part_copy(kind, step, kh).start()

    def return_part(step, kh):
        kg = group_at(step)
        for kind in (1, 0):
            part_copy(kind, step, kh).wait_recv()
            total = part[kind, step, kh, core] + sib_got[kind, step, kh].astype(F32)
            for n in range(2):
                ret_send[kind, kh, 2 * kg + n] = total[n].astype(BF16)
                start_copy(place, *ret_args(kind, 2 * kg + n, kh))

    def return_queries(qg, qh):
        grad_q = (dqt[qh, qg] * SCALE).T.astype(BF16).reshape(4, HALF, HEAD)
        for n in range(4):
            ret_send[2, qh, 4 * qg + n] = grad_q[n]
            start_copy(place, *ret_args(2, 4 * qg + n, qh))

    mean_send[...] = jnp.zeros_like(mean_send)
    dqt[...] = jnp.zeros_like(dqt)
    pass_on(KEY, 0)
    wait_rows(QUERY, 0)
    wait_passed(KEY, 0)
    scores(0, 0)
    pass_on(VALUE, 0)
    turn_keys(0)
    wait_passed(VALUE, 0)
    mix(0)
    send_stats(0)
    wait_rows(QUERY, 1)
    scores(1, 0)
    pass_on(KEY, 1)
    grads_of_mixed(0)
    wait_passed(KEY, 1)
    scores(1, 1)
    pass_on(VALUE, 1)
    for i in range(8):
        start_copy(place, *o_args(i, 0))
    back_lower()
    wait_passed(VALUE, 1)
    mix(1)
    send_stats(1)
    for i in range(8):
        start_copy(place, *mean_args(i))
        start_copy(place, *o_args(i, 1))
    return_queries(0, 0)
    return_queries(1, 0)
    turn_keys(1)
    for n in range(1, 4):
        wait_arrived(go_all.at[(dp + 8 - 2 * n) % 8], zrecv.at[n - 1])
        go_across(n).start()
    grads_of_mixed(1)

    def gated_copy(n):
        there = (dp + n) % 8
        cols = pl.ds(pl.multiple_of(there * 128, 128), 128)
        return pltpu.make_async_remote_copy(
            gated_buf.at[:, cols], gd_got.at[dp], gdsend, gdrecv,
            device_id={"dp": there},
        )

    def gate():
        wait_arrived(mean_got, mrecv)
        for half in range(2):
            wait_arrived(mixed_got.at[half], orecv.at[half])
        means = mean_got[...].reshape(HEADS, 256).T
        means = jnp.concatenate([means[0:HALF], means[128 : 128 + HALF]], axis=0)
        mixed = jnp.concatenate(
            [
                flat(mixed_got[:, head]).astype(F32) + means[:, head : head + 1]
                for head in range(HEADS)
            ],
            axis=1,
        )
        mixed_n, _ = norm_rows(mixed)
        gated_buf[...] = (mixed_n * u_buf[...].astype(F32)).astype(BF16)
        for n in range(1, 8):
            gated_copy(n).start()
        gd_got[dp] = gated_buf[:, pl.ds(pl.multiple_of(dp * 128, 128), 128)]
        gpre_buf[...] = (gate_buf[...] * mixed_n * slope_buf[:, U_COL : U_COL + D]).astype(BF16)

    def to_ctx(n):
        there = (t + n) % CTX
        return pltpu.make_async_remote_copy(
            c_send.at[there], c_got.at[n - 1], csend, crecv,
            device_id={"ctx": there},
        )

    def product():
        for n in range(4):
            wait_arrived(go_all.at[(place.sibling["dp"] + 8 - 2 * n) % 8], gfrecv.at[n])
        wait_arrived(gd_got.at[0:7], gdrecv)
        total = dot_tn(gd_got[...].reshape(8 * ROWS, 128), go_all[...].reshape(8 * ROWS, D)).T
        total = total.reshape(8, CTX, 8, 128)
        for there in range(CTX):
            piece = total[:, there].reshape(64, 128)
            g_buf[there] = piece
            c_send[there] = piece.astype(BF16)
        for n in range(1, CTX):
            to_ctx(n).start()

    def fin_copy(n):
        there = (dp + n) % 8
        return pltpu.make_async_remote_copy(
            f_send.at[there], f_got.at[dp], fin_send, fin_recv,
            device_id={"dp": there},
        )

    def sum_places():
        wait_arrived(c_got, crecv)
        total = g_buf[t]
        for n in range(1, CTX):
            total = total + c_got[n - 1].astype(F32)
        f_send[...] = (total * (24576.0 ** (-0.5))).reshape(8, 8, 128)
        for n in range(1, 8):
            fin_copy(n).start()
        f_got[dp] = f_send[dp]

    back_part(0, 0)
    back_part(0, 1)
    return_part(0, 0)
    gate()
    back_part(1, 0)
    return_part(0, 1)
    back_part(1, 1)
    return_part(1, 0)
    back_part(2, 0)
    return_part(1, 1)
    back_part(2, 1)
    return_part(2, 0)
    product()
    back_part(3, 0)
    return_part(2, 1)
    back_part(3, 1)
    return_part(3, 0)
    return_queries(0, 1)
    return_queries(1, 1)
    return_part(3, 1)

    layer_out[...] = (dot_nn(gated_buf[...], w_out[...]) + tokens[...].astype(F32)).astype(BF16)
    rows_acc[...] = dot_nt(gpre_buf[...], w_buf[:, U_COL : U_COL + D])

    def rows_part(kind, col):
        for half in range(2):
            wait_arrived(ret_got.at[kind, half], rrecv.at[kind, half])
        gradient = jnp.concatenate([flat(ret_got[kind, :, head]) for head in range(HEADS)], axis=1)
        grad_pre = (gradient.astype(F32) * slope_buf[:, col : col + D]).astype(BF16)
        rows_acc[...] += dot_nt(grad_pre, w_buf[:, col : col + D])

    rows_part(1, V_COL)
    sum_places()
    rows_part(0, K_COL)
    rows_part(2, Q_COL)

    normed, inv_x = norm_rows(tokens[...].astype(F32))
    grad_tokens[...] = (
        go_all[dp].astype(F32) + norm_back(rows_acc[...], normed, inv_x)
    ).astype(BF16)

    wait_arrived(f_got.at[0:7], fin_recv)
    for n in range(8):
        out_grad[:, n * 128 : (n + 1) * 128] = f_got[n]

    for n in range(1, 4):
        go_along(n).wait_send()
    for n in range(4):
        go_across(n).wait_send()
    wait_sent(place, gd_got.at[0:7], gdsend)
    wait_sent(place, f_got.at[0:7], fin_send)
    wait_sent(place, c_got, csend)
    hist_forward().wait_send()
    wait_sent_eight(place, hist_all.at[core], hsend)
    wait_sent_eight(place, mean_send, msend)
    for half in range(2):
        wait_sent(place, stats.at[0:7, half], ssend.at[half])
        wait_sent_eight(place, o_send.at[half], osend.at[half])
        for kind in range(4):
            wait_sent_eight(place, send_buf.at[kind, half], send_sem.at[kind, half])
        for kind in range(3):
            wait_sent_eight(place, ret_send.at[kind, half], rsend.at[kind, half])
        for kind in (KEY, VALUE):
            for batch in range(2):
                forward(kind, half, batch).wait_send()
    for kind in range(2):
        for kg in range(4):
            for kh in range(2):
                part_copy(kind, kg, kh).wait_send()


def copy_kernel(*refs):
    for source, target in zip(refs[:3], refs[3:]):
        target[...] = source[...]


def copied(arrays):
    vmem_spec = pl.BlockSpec(memory_space=pltpu.VMEM)
    return pl.pallas_call(
        copy_kernel,
        out_shape=tuple(jax.ShapeDtypeStruct(a.shape, a.dtype) for a in arrays),
        in_specs=[vmem_spec] * 3,
        out_specs=(vmem_spec,) * 3,
        name="results",
    )(*arrays)


def on_device(tokens, segments, w_in, w_out, grad_out):
    any_spec = pl.BlockSpec(memory_space=pl.ANY)
    vmem_spec = pl.BlockSpec(memory_space=pltpu.VMEM)
    dma = pltpu.SemaphoreType.DMA
    vmem = pltpu.VMEM
    tiles = len(TILES)
    results = pl.pallas_call(
        layer_kernel,
        out_shape=(
            jax.ShapeDtypeStruct((ROWS, D), BF16),
            jax.ShapeDtypeStruct((ROWS, D), BF16),
            jax.ShapeDtypeStruct((8, D), F32),
        ),
        in_specs=[any_spec, vmem_spec, any_spec, any_spec, any_spec],
        out_specs=(vmem_spec, vmem_spec, vmem_spec),
        scratch_shapes=[
            vmem((ROWS, D), BF16),
            vmem((8, ROWS, D), BF16),
            vmem((D, 4 * D), BF16),
            vmem((D, D), BF16),
            vmem((ROWS, D), BF16),
            vmem((ROWS, 4 * D), F32),
            vmem((ROWS, D), BF16),
            vmem((ROWS, D), F32),
            vmem((1, 256), jnp.int32),
            vmem((2, 8, 1, 256), jnp.int32),
            vmem((2, 4, G, 128), F32),
            vmem((2, 2, 1, G), F32),
            vmem((4, 2, HEADS, HALF, HEAD), BF16),
            vmem((2, 2, 8, HALF, HEAD), BF16),
            vmem((2, 2, 8, HALF, HEAD), BF16),
            vmem((2, 8, HALF, HEAD), BF16),
            vmem((2, 8, HALF, HEAD), BF16),
            vmem((tiles, G, G), BF16),
            vmem((tiles, G, G), BF16),
            vmem((2, 4, HEAD, G), BF16),
            vmem((2, 4, HEAD, G), BF16),
            vmem((2, 2, HEAD, G), F32),
            vmem((2, 2, HEAD, G), BF16),
            vmem((2, 8, HALF, HEAD), BF16),
            vmem((2, HEADS, HALF, HEAD), BF16),
            vmem((8, 1, 256), F32),
            vmem((HEADS, 1, 256), F32),
            vmem((HEADS, 2, 8, G), F32),
            vmem((2, 2, HEAD, G), BF16),
            vmem((2, 2, HEAD, G), F32),
            vmem((2, 4, G, HEAD), F32),
            vmem((2, G, HEAD), F32),
            vmem((2, 4, 2, 2, 2, HALF, HEAD), F32),
            vmem((2, 4, 2, 2, HALF, HEAD), BF16),
            vmem((2, 4, 2, 2, HALF, HEAD), BF16),
            vmem((3, 2, 8, HALF, HEAD), BF16),
            vmem((3, 2, HEADS, HALF, HEAD), BF16),
            vmem((ROWS, D), F32),
            vmem((ROWS, D), BF16),
            vmem((ROWS, D), BF16),
            vmem((8, ROWS, 128), BF16),
            vmem((CTX, 64, 128), F32),
            vmem((CTX, 64, 128), BF16),
            vmem((CTX - 1, 64, 128), BF16),
            vmem((8, 8, 128), F32),
            vmem((8, 8, 128), F32),
            dma((3,)), dma((8,)),
            dma, dma, dma, dma,
            dma((4, 2)), dma((4, 2, 2)), dma((2, 2, 2)), dma((2, 2, 2)),
            dma((2,)), dma((2,)), dma, dma,
            dma((2,)), dma((2,)),
            dma((2, 4, 2)), dma((2, 4, 2)), dma((3, 2)), dma((3, 2)),
            dma((3,)), dma((3,)), dma((4,)), dma((4,)),
            dma, dma, dma, dma,
            dma, dma,
        ],
        compiler_params=pltpu.CompilerParams(
            collective_id=0, has_side_effects=True, vmem_limit_bytes=VMEM_LIMIT
        ),
        name="layer",
    )(tokens, segments, w_in, w_out, grad_out)
    return copied(results)


def solution(mesh):
    return jax.shard_map(
        on_device,
        mesh=mesh,
        in_specs=(P(("dp", "ctx"), None), P("dp", "ctx"), P(), P(), P(("dp", "ctx"), None)),
        out_specs=(P(("dp", "ctx"), None), P(("dp", "ctx"), None), P(("dp", "ctx"), None)),
        check_vma=False,
    )
```

```python
import jax
import jax.numpy as jnp
from jax import lax
from jax.experimental import pallas as pl
from jax.experimental.pallas import tpu as pltpu
from jax.sharding import PartitionSpec as P

HEADS = 8
HEAD = 128
ROWS = 192
HALF = 96
D = 1024
CTX = 16
G = 4 * HALF
EPS = 1e-05
SCALE = HEAD ** (-0.5)
FAR = -float(2**30)
VMEM_LIMIT = 60 * 1024 * 1024
F32 = jnp.float32
BF16 = jnp.bfloat16
U_COL, V_COL, Q_COL, K_COL = 0, D, 2 * D, 3 * D
KEY, QUERY, VALUE, GNORM = 0, 1, 2, 3

TILES = [(0, 0, 0, 0), (0, 0, 0, 1)]
TILES += [(1, 0, 0, g) for g in range(4)] + [(1, 0, 1, g) for g in range(4)]
TILES += [(0, 1, 0, g) for g in range(4)]
TILES += [(1, 1, 0, g) for g in range(4)] + [(1, 1, 1, g) for g in (2, 3)]
FIRST = {(0, 0, 0): 0, (1, 0, 0): 2, (1, 0, 1): 6, (0, 1, 0): 10, (1, 1, 0): 14, (1, 1, 1): 16}


def norm_rows(matrix):
    average = jnp.mean(matrix, axis=-1, keepdims=True)
    centred = matrix - average
    inverse = lax.rsqrt(jnp.mean(centred * centred, axis=-1, keepdims=True) + EPS)
    return centred * inverse, inverse


def norm_back(gradient, normed, inverse):
    first = jnp.mean(gradient, axis=-1, keepdims=True)
    second = jnp.mean(gradient * normed, axis=-1, keepdims=True)
    return (gradient - first - normed * second) * inverse


def dot_nt(left, right):
    return lax.dot_general(left, right, (((1,), (1,)), ((), ())), preferred_element_type=F32)


def dot_tn(left, right):
    return lax.dot_general(left, right, (((0,), (0,)), ((), ())), preferred_element_type=F32)


def dot_nn(left, right):
    return lax.dot_general(left, right, (((1,), (0,)), ((), ())), preferred_element_type=F32)


def flat(blocks):
    return blocks.reshape(-1, HEAD)


class Place:
    def __init__(self):
        self.dp = lax.axis_index("dp")
        self.t = lax.axis_index("ctx")
        self.plane = 2 * (self.dp // 2)
        self.core = self.dp % 2
        self.z = self.dp // 2
        self.sibling = {"dp": self.plane + 1 - self.core}
        self.head = self.t % HEADS
        self.slot = self.t // 2

    def worker(self, head):
        return self.plane + self.t % 2, self.core * HEADS + head

    def owner(self, i):
        return self.plane + self.t // HEADS, 2 * i + self.core

    def is_me(self, device):
        return (device[0] == self.dp) & (device[1] == self.t)

    def has_self(self):
        return (self.t % 2 == self.core) & (self.t // HEADS == self.core)


def ident(device):
    return {"dp": device[0], "ctx": device[1]}


def signal_if_other(place, barrier, device):
    @pl.when(jnp.logical_not(place.is_me(device)))
    def _():
        pl.semaphore_signal(barrier, inc=1, device_id=ident(device))


def send(device, src, dst, send_sem, recv_sem):
    pltpu.make_async_remote_copy(src, dst, send_sem, recv_sem, device_id=ident(device)).start()


def keep(device, src, dst, send_sem, recv_sem):
    pltpu.make_async_copy(src, dst, recv_sem).start()


def send_eight(place, first, args):
    @pl.when(place.has_self())
    def _():
        keep(*args(first))

    @pl.when(jnp.logical_not(place.has_self()))
    def _():
        send(*args(first))

    for n in range(1, 8):
        send(*args((first + n) % 8))


def wait_sent(place, ref, sem):
    pltpu.make_async_remote_copy(ref, ref, sem, sem, device_id=place.sibling).wait_send()


def wait_sent_eight(place, ref, sem):
    @pl.when(place.has_self())
    def _():
        wait_sent(place, ref.at[0:7], sem)

    @pl.when(jnp.logical_not(place.has_self()))
    def _():
        wait_sent(place, ref, sem)


def wait_arrived(dst, recv_sem):
    pltpu.make_async_copy(dst, dst, recv_sem).wait()


def history_masks(hist_all, k_hist, q_hist, core):
    lane = lax.broadcasted_iota(jnp.int32, (G, 128), 1).astype(F32)

    def numbers(blocks):
        rows = jnp.broadcast_to(
            jnp.concatenate(blocks, axis=1).astype(F32).astype(BF16), (16, G)
        )
        return dot_tn(rows, jnp.full((16, 128), 1.0 / 16, BF16))

    for half in range(2):
        lanes = slice(half * 128, half * 128 + HALF)
        for g in range(4):
            number = numbers([hist_all[n // 2, 2 * g + n % 2, :, lanes] for n in range(4)])
            other = (lane < 8.0) & (number != lane)
            k_hist[half, g] = jnp.where(other, FAR, 0.0).astype(BF16)
        for g in range(2):
            number = numbers([hist_all[core, 4 * g + n, :, lanes] for n in range(4)])
            q_hist[half, g] = jnp.where(number == lane, 1.0, 0.0).astype(BF16)


def query_positions(half, g, core):
    lane = lax.broadcasted_iota(jnp.int32, (1, G), 1)
    inside = lane // HALF
    block = 8 * g + 2 * inside + core
    return (31 - block if half else block) * HALF + lane - inside * HALF


def key_positions(half, g):
    row = lax.broadcasted_iota(jnp.int32, (G, 128), 0)
    inside = row // HALF
    block = 4 * g + 2 * (inside % 2) + inside // 2
    return (31 - block if half else block) * HALF + row - inside * HALF


def key_rows(got, half, g):
    return jnp.concatenate([flat(got[half, n, pl.ds(2 * g, 2)]) for n in range(2)], axis=0)


def three(matrix):
    return jnp.concatenate([matrix, matrix, matrix], axis=1)


def score_tile(n, q_got, k_got, k_hist, q_hist, p_buf, s_buf, core):
    qh, qg, kh, kg = TILES[n]
    keys = jnp.concatenate([key_rows(k_got, kh, kg), k_hist[kh, kg]], axis=1)
    queries = jnp.concatenate([flat(q_got[qh, 4 * qg : 4 * qg + 4]), q_hist[qh, qg]], axis=1)
    half = dot_nt(keys, queries) * (0.5 * SCALE)
    up = 1.0 + jnp.tanh(half)
    weights = half * up
    slope = up + weights * (2.0 - up)
    if qh == kh and kg // 2 == qg:
        visible = three(key_positions(kh, kg)) <= query_positions(qh, qg, core)
        weights = jnp.where(visible, weights, 0.0)
        slope = jnp.where(visible, slope, 0.0)
    p_buf[n] = weights.astype(BF16)
    s_buf[n] = slope.astype(BF16)


def mix_tiles(qh, qg, kh, vt, p_buf):
    total = None
    for n, tile in enumerate(TILES):
        if tile[:3] == (qh, qg, kh):
            part = dot_nn(vt[tile[2], tile[3]], p_buf[n])
            total = part if total is None else total + part
    return total


def back_tile(tile, n, q_got, v_got, kt, dot_buf, p_buf, s_buf, dqt):
    qh, qg, kh, kg = tile
    grads = dot_buf[qh, qg]
    grad_scores = dot_nn(key_rows(v_got, kh, kg), grads) * s_buf[n].astype(F32)
    grad_scores = grad_scores.astype(BF16)
    grad_v = dot_nt(p_buf[n], grads)
    grad_k = dot_nn(grad_scores, flat(q_got[qh, 4 * qg : 4 * qg + 4]))
    dqt[qh, qg] += dot_nn(kt[kh, kg], grad_scores)
    return grad_k, grad_v


def layer_kernel(
    tokens_in, hist, w_in, w_out_in, grad_out_in,
    layer_out, grad_tokens, out_grad,
    tokens, go_all, w_buf, w_out, normed_buf, slope_buf, u_buf, gate_buf,
    hist_buf, hist_all, k_hist, q_hist,
    send_buf, k_got, v_got, q_got, n_got,
    p_buf, s_buf, vt, kt, ot_buf, gt_buf, o_send, mixed_got, mean_send, mean_got, stats, dot_buf, dqt,
    low_buf, grads_buf, part, part_send, sib_got, ret_send, ret_got, rows_acc,
    gated_buf, gpre_buf, gd_got, g_buf, c_send, c_got, f_send, f_got,
    in_sem, w_sem, hsend, hrecv, hfsend, hfrecv, send_sem, recv_sem, fsend, frecv,
    osend, orecv, msend, mrecv, ssend, srecv, psend, precv, rsend, rrecv,
    zsend, zrecv, gfsend, gfrecv, gdsend, gdrecv, csend, crecv, fin_send, fin_recv,
):
    place = Place()
    core, t, z, my_head, slot, dp = place.core, place.t, place.z, place.head, place.slot, place.dp

    t_copy = pltpu.make_async_copy(tokens_in, tokens, in_sem.at[0])
    t_copy.start()
    chunks = [K_COL, K_COL + 512, Q_COL, Q_COL + 512, V_COL, V_COL + 512, U_COL, U_COL + 512]

    def w_copy(n):
        cols = pl.ds(chunks[n], 512)
        return pltpu.make_async_copy(w_in.at[:, cols], w_buf.at[:, cols], w_sem.at[n])

    for n in range(2):
        w_copy(n).start()
    go_copy = pltpu.make_async_copy(grad_out_in, go_all.at[dp], in_sem.at[1])
    go_copy.start()
    for n in range(2, 8):
        w_copy(n).start()
    wo_copy = pltpu.make_async_copy(w_out_in, w_out, in_sem.at[2])
    wo_copy.start()

    barrier = pltpu.get_barrier_semaphore()
    for n in range(8):
        signal_if_other(place, barrier, place.owner(n))
        signal_if_other(place, barrier, place.worker(n))
    for n in range(1, 8):
        pl.semaphore_signal(barrier, inc=1, device_id={"dp": (dp + n) % 8})
    for n in range(1, CTX):
        pl.semaphore_signal(barrier, inc=1, device_id={"ctx": (t + n) % CTX})

    hist_buf[...] = jnp.zeros_like(hist_buf)
    hist_buf[:, 0:HALF] = hist[:, 0:HALF]
    hist_buf[:, 128 : 128 + HALF] = hist[:, HALF:ROWS]
    t_copy.wait()
    normed_buf[...] = norm_rows(tokens[...].astype(F32))[0].astype(BF16)

    def send_args(kind, head, half):
        got = (k_got, q_got, v_got, n_got)[kind]
        dst = got.at[half, t % 2, slot] if kind in (KEY, VALUE) else got.at[half, slot]
        batch = slot // 4 if kind in (KEY, VALUE) else 0
        return (
            place.worker(head), send_buf.at[kind, half, head], dst,
            send_sem.at[kind, half], recv_sem.at[kind, half, batch],
        )

    def hist_args(head):
        return place.worker(head), hist_buf, hist_all.at[t % 2, slot], hsend, hrecv

    def go_along(n):
        ref = go_all.at[dp]
        return pltpu.make_async_remote_copy(
            ref, ref, zsend.at[n - 1], zrecv.at[n - 1], device_id={"dp": (dp + 2 * n) % 8}
        )

    def go_across(n):
        ref = go_all.at[(dp + 8 - 2 * n) % 8]
        return pltpu.make_async_remote_copy(
            ref, ref, gfsend.at[n], gfrecv.at[n], device_id=place.sibling
        )

    def project(n):
        w_copy(n).wait()
        cols = slice(chunks[n], chunks[n] + 512)
        half = 0.5 * dot_nn(normed_buf[...], w_buf[:, cols])
        up = 1.0 + jnp.tanh(half)
        act = half * up
        slope_buf[:, cols] = act + (0.5 * up) * (1.0 - act)
        return act.astype(BF16)

    for n in range(8):
        act = project(n)
        if n == 0:
            pl.semaphore_wait(barrier, 16 + 7 + 15 - 2 * place.has_self().astype(jnp.int32))
            send_eight(place, my_head, hist_args)
        if n < 6:
            for j in range(4):
                head = (n % 2) * 4 + j
                for half in range(2):
                    send_buf[n // 2, half, head] = act[
                        half * HALF : (half + 1) * HALF, j * 128 : (j + 1) * 128
                    ]
            if n % 2:
                send_eight(place, my_head, lambda head: send_args(n // 2, head, 0))
        else:
            u_buf[:, chunks[n] : chunks[n] + 512] = act

    go_copy.wait()
    wo_copy.wait()
    gate_buf[...] = dot_nt(go_all[dp], w_out[...])
    grad_norm = (gate_buf[...] * u_buf[...].astype(F32)).astype(BF16)
    for head in range(HEADS):
        for half in range(2):
            send_buf[GNORM, half, head] = grad_norm[
                half * HALF : (half + 1) * HALF, head * 128 : (head + 1) * 128
            ]
    send_eight(place, my_head, lambda head: send_args(GNORM, head, 0))
    for kind in (QUERY, KEY, VALUE, GNORM):
        send_eight(place, my_head, lambda head: send_args(kind, head, 1))
    for n in (2, 1, 3):
        go_along(n).start()
    go_across(0).start()

    def hist_forward():
        ref = hist_all.at[core]
        return pltpu.make_async_remote_copy(ref, ref, hfsend, hfrecv, device_id=place.sibling)

    def forward(kind, half, batch):
        ref = (k_got, None, v_got)[kind].at[half, core, 4 * batch : 4 * batch + 4]
        return pltpu.make_async_remote_copy(
            ref, ref, fsend.at[kind // 2, half, batch], frecv.at[kind // 2, half, batch],
            device_id=place.sibling,
        )

    def pass_on(kind, half):
        got = (k_got, None, v_got)[kind]
        for batch in range(2):
            wait_arrived(
                got.at[half, core, 4 * batch : 4 * batch + 4], recv_sem.at[kind, half, batch]
            )
            forward(kind, half, batch).start()

    def wait_passed(kind, half):
        for batch in range(2):
            forward(kind, half, batch).wait_recv()

    def wait_rows(kind, half):
        got = (None, q_got, None, n_got)[kind]
        wait_arrived(got.at[half], recv_sem.at[kind, half, 0])

    wait_arrived(hist_all.at[core], hrecv)
    hist_forward().start()
    hist_forward().wait_recv()
    history_masks(hist_all, k_hist, q_hist, core)

    def scores(qh, kh):
        for n, tile in enumerate(TILES):
            if (tile[0], tile[2]) == (qh, kh):
                score_tile(n, q_got, k_got, k_hist, q_hist, p_buf, s_buf, core)

    def mean_args(i):
        return place.owner(i), mean_send.at[i], mean_got.at[my_head], msend, mrecv

    def o_args(i, half):
        return (
            place.owner(i), o_send.at[half, i], mixed_got.at[half, my_head],
            osend.at[half], orecv.at[half],
        )

    def mix(qh):
        for g in range(4):
            vt[qh, g] = key_rows(v_got, qh, g).T
        for qg in range(2):
            mixed_t = mix_tiles(qh, qg, qh, vt, p_buf)
            if qh == 1:
                mixed_t = mixed_t + ot_buf[qh, qg]
            average = jnp.mean(mixed_t, axis=0, keepdims=True)
            centred = mixed_t - average
            ot_buf[qh, qg] = centred
            o_send[qh, 4 * qg : 4 * qg + 4] = centred.T.astype(BF16).reshape(4, HALF, HEAD)
            for n in range(4):
                mean_send[4 * qg + n, :, qh * 128 : qh * 128 + HALF] = average[
                    :, n * HALF : (n + 1) * HALF
                ]
            stats[my_head, qh, 4 * qg : 4 * qg + 1] = average
            stats[my_head, qh, 4 * qg + 1 : 4 * qg + 2] = jnp.sum(
                centred * centred, axis=0, keepdims=True
            )

    def stats_copy(qh, n):
        there = (t // HEADS) * HEADS + (my_head + n) % HEADS
        ref = stats.at[my_head, qh]
        return pltpu.make_async_remote_copy(
            ref, ref, ssend.at[qh], srecv.at[qh], device_id={"ctx": there}
        )

    def send_stats(qh):
        wait_rows(GNORM, qh)
        for qg in range(2):
            grad_t = flat(n_got[qh, 4 * qg : 4 * qg + 4]).T
            gt_buf[qh, qg] = grad_t
            grad_t = grad_t.astype(F32)
            stats[my_head, qh, 4 * qg + 2 : 4 * qg + 3] = jnp.sum(grad_t, axis=0, keepdims=True)
            stats[my_head, qh, 4 * qg + 3 : 4 * qg + 4] = jnp.sum(
                grad_t * ot_buf[qh, qg], axis=0, keepdims=True
            )
        for n in range(1, HEADS):
            stats_copy(qh, n).start()

    def grads_of_mixed(qh):
        wait_arrived(stats.at[0:7, qh], srecv.at[qh])
        for qg in range(2):
            rows = [
                [stats[h, qh, 4 * qg + k : 4 * qg + k + 1] for h in range(HEADS)] for k in range(4)
            ]
            average = sum(rows[0]) * (1.0 / HEADS)
            off = [row - average for row in rows[0]]
            spread = sum(rows[1]) + HEAD * sum(o * o for o in off)
            inverse = lax.rsqrt(spread * (1.0 / D) + EPS)
            first = sum(rows[2]) * (1.0 / D)
            second = (sum(rows[3]) + sum(o * a for o, a in zip(off, rows[2]))) * (1.0 / D)
            centred = ot_buf[qh, qg] + (stats[my_head, qh, 4 * qg : 4 * qg + 1] - average)
            dot_buf[qh, qg] = (
                (gt_buf[qh, qg].astype(F32) - first - centred * (second * inverse * inverse))
                * inverse
            ).astype(BF16)

    def turn_keys(half):
        for g in range(4):
            kt[half, g] = key_rows(k_got, half, g).T

    def part_copy(kind, kg, kh):
        ref = part_send.at[kind, kg, kh]
        return pltpu.make_async_remote_copy(
            ref, sib_got.at[kind, kg, kh], psend.at[kind, kg, kh], precv.at[kind, kg, kh],
            device_id=place.sibling,
        )

    def ret_args(kind, i, half):
        return (
            place.owner(i), ret_send.at[kind, half, i], ret_got.at[kind, half, my_head],
            rsend.at[kind, half], rrecv.at[kind, half],
        )

    def back(qh, qg, kh, kg):
        n = FIRST[qh, qg, kh] + kg
        return back_tile(
            (qh, qg, kh, kg), n, q_got, v_got, kt, dot_buf, p_buf, s_buf, dqt
        )

    def back_lower():
        for kg in range(4):
            grad_k, grad_v = back(0, 1, 0, kg)
            if kg < 2:
                term_k, term_v = back(0, 0, 0, kg)
                grad_k, grad_v = grad_k + term_k, grad_v + term_v
            low_buf[0, kg], low_buf[1, kg] = grad_k, grad_v

    def group_at(step):
        return (step + t) % 4

    def back_part(step, kh):
        kg = group_at(step)
        grad_k, grad_v = back(1, 0, kh, kg)
        if kh == 0:
            term_k, term_v = back(1, 1, kh, kg)
            grads_buf[0] = ((grad_k + term_k) + low_buf[0, kg]).reshape(2, ROWS, HEAD)
            grads_buf[1] = ((grad_v + term_v) + low_buf[1, kg]).reshape(2, ROWS, HEAD)
        else:
            grads_buf[0] = grad_k.reshape(2, ROWS, HEAD)
            grads_buf[1] = grad_v.reshape(2, ROWS, HEAD)

            @pl.when(kg >= 2)
            def _():
                term_k, term_v = back(1, 1, kh, kg)
                grads_buf[0] += term_k.reshape(2, ROWS, HEAD)
                grads_buf[1] += term_v.reshape(2, ROWS, HEAD)

        for kind in (1, 0):
            scale = 0.5 * SCALE if kind == 0 else 1.0
            part_send[kind, step, kh] = (
                (grads_buf[kind, 1 - core] * scale).astype(BF16).reshape(2, HALF, HEAD)
            )
            part_copy(kind, step, kh).start()
            part[kind, step, kh] = (grads_buf[kind, core] * scale).reshape(2, HALF, HEAD)

    def return_part(step, kh):
        kg = group_at(step)
        for kind in (1, 0):
            part_copy(kind, step, kh).wait_recv()
            total = part[kind, step, kh] + sib_got[kind, step, kh].astype(F32)
            for n in range(2):
                ret_send[kind, kh, 2 * kg + n] = total[n].astype(BF16)
        first, second = 2 * kg + slot % 2, 2 * kg + 1 - slot % 2
        own = place.has_self() & (kg == slot // 2)

        @pl.when(own)
        def _():
            for kind in (1, 0):
                keep(*ret_args(kind, first, kh))

        @pl.when(jnp.logical_not(own))
        def _():
            for kind in (1, 0):
                send(*ret_args(kind, first, kh))

        for kind in (1, 0):
            send(*ret_args(kind, second, kh))

    def return_queries(qh):
        for qg in range(2):
            grad_q = (dqt[qh, qg] * (0.5 * SCALE)).T.astype(BF16).reshape(4, HALF, HEAD)
            for n in range(4):
                ret_send[2, qh, 4 * qg + n] = grad_q[n]
        send_eight(place, slot, lambda i: ret_args(2, i, qh))

    def pass_grads(n):
        wait_arrived(go_all.at[(dp + 8 - 2 * n) % 8], zrecv.at[n - 1])
        go_across(n).start()

    mean_send[...] = jnp.zeros_like(mean_send)
    dqt[...] = jnp.zeros_like(dqt)
    pass_on(KEY, 0)
    wait_rows(QUERY, 0)
    wait_passed(KEY, 0)
    scores(0, 0)
    pass_on(VALUE, 0)
    turn_keys(0)
    wait_passed(VALUE, 0)
    mix(0)
    send_stats(0)
    wait_rows(QUERY, 1)
    scores(1, 0)
    pass_on(KEY, 1)
    grads_of_mixed(0)
    wait_passed(KEY, 1)
    scores(1, 1)
    pass_grads(2)
    turn_keys(1)
    for qg in range(2):
        ot_buf[1, qg] = mix_tiles(1, qg, 0, vt, p_buf)
    back_lower()
    pass_on(VALUE, 1)
    wait_passed(VALUE, 1)
    mix(1)
    send_stats(1)
    send_eight(place, slot, mean_args)
    for half in range(2):
        send_eight(place, slot, lambda i: o_args(i, half))
    return_queries(0)
    for n in (1, 3):
        pass_grads(n)
    grads_of_mixed(1)

    def gated_copy(n):
        there = (dp + n) % 8
        cols = pl.ds(pl.multiple_of(there * 128, 128), 128)
        return pltpu.make_async_remote_copy(
            gated_buf.at[:, cols], gd_got.at[dp], gdsend, gdrecv,
            device_id={"dp": there},
        )

    def gate():
        wait_arrived(mean_got, mrecv)
        for half in range(2):
            wait_arrived(mixed_got.at[half], orecv.at[half])
        means = mean_got[...].reshape(HEADS, 256).T
        means = jnp.concatenate([means[0:HALF], means[128 : 128 + HALF]], axis=0)
        mixed = jnp.concatenate(
            [
                flat(mixed_got[:, head]).astype(F32) + means[:, head : head + 1]
                for head in range(HEADS)
            ],
            axis=1,
        )
        mixed_n, _ = norm_rows(mixed)
        gated_buf[...] = (mixed_n * u_buf[...].astype(F32)).astype(BF16)
        for n in range(1, 8):
            gated_copy(n).start()
        gd_got[dp] = gated_buf[:, pl.ds(pl.multiple_of(dp * 128, 128), 128)]
        gpre_buf[...] = (gate_buf[...] * mixed_n * slope_buf[:, U_COL : U_COL + D]).astype(BF16)

    def to_ctx(n):
        there = (t + n) % CTX
        return pltpu.make_async_remote_copy(
            c_send.at[there], c_got.at[n - 1], csend, crecv,
            device_id={"ctx": there},
        )

    def fin_copy(n):
        there = (dp + n) % 8
        return pltpu.make_async_remote_copy(
            f_send.at[there], f_got.at[dp], fin_send, fin_recv, device_id={"dp": there}
        )

    def product():
        for n in range(4):
            wait_arrived(go_all.at[(place.sibling["dp"] + 8 - 2 * n) % 8], gfrecv.at[n])
        wait_arrived(gd_got.at[0:7], gdrecv)
        total = dot_tn(gd_got[...].reshape(8 * ROWS, 128), go_all[...].reshape(8 * ROWS, D)).T
        f_send[...] = total.reshape(8, 128, 128).astype(BF16)
        for n in range(1, 8):
            fin_copy(n).start()

    def spread():
        wait_arrived(f_got.at[0:7], fin_recv)
        f_got[dp] = f_send[dp]
        total = f_got[...].astype(F32).reshape(8, CTX, 8, 128)
        for there in range(CTX):
            piece = total[:, there].reshape(64, 128)
            g_buf[there] = piece
            c_send[there] = piece.astype(BF16)
        for n in range(1, CTX):
            to_ctx(n).start()

    def sum_places():
        wait_arrived(c_got, crecv)
        total = g_buf[t]
        for n in range(1, CTX):
            total = total + c_got[n - 1].astype(F32)
        total = total * (24576.0 ** (-0.5))
        for n in range(8):
            out_grad[:, n * 128 : (n + 1) * 128] = total[8 * n : 8 * n + 8]

    back_part(0, 0)
    back_part(0, 1)
    return_part(0, 0)
    back_part(1, 0)
    return_part(0, 1)
    gate()
    back_part(1, 1)
    return_part(1, 0)
    back_part(2, 0)
    return_part(1, 1)
    back_part(2, 1)
    back_part(3, 0)
    return_part(2, 0)
    back_part(3, 1)
    return_part(2, 1)
    return_queries(1)
    return_part(3, 0)
    product()
    return_part(3, 1)

    layer_out[...] = (dot_nn(gated_buf[...], w_out[...]) + tokens[...].astype(F32)).astype(BF16)
    rows_acc[...] = dot_nt(gpre_buf[...], w_buf[:, U_COL : U_COL + D])

    def rows_part(kind, col):
        for half in range(2):
            wait_arrived(ret_got.at[kind, half], rrecv.at[kind, half])
        gradient = jnp.concatenate([flat(ret_got[kind, :, head]) for head in range(HEADS)], axis=1)
        grad_pre = (gradient.astype(F32) * slope_buf[:, col : col + D]).astype(BF16)
        rows_acc[...] += dot_nt(grad_pre, w_buf[:, col : col + D])

    spread()
    rows_part(1, V_COL)
    rows_part(0, K_COL)
    rows_part(2, Q_COL)

    normed, inv_x = norm_rows(tokens[...].astype(F32))
    grad_tokens[...] = (
        go_all[dp].astype(F32) + norm_back(rows_acc[...], normed, inv_x)
    ).astype(BF16)

    sum_places()

    for n in range(1, 4):
        go_along(n).wait_send()
    for n in range(4):
        go_across(n).wait_send()
    wait_sent(place, gd_got.at[0:7], gdsend)
    wait_sent(place, f_got.at[0:7], fin_send)
    wait_sent(place, c_got, csend)
    hist_forward().wait_send()
    wait_sent_eight(place, hist_all.at[core], hsend)
    wait_sent_eight(place, mean_send, msend)
    for half in range(2):
        wait_sent(place, stats.at[0:7, half], ssend.at[half])
        wait_sent_eight(place, o_send.at[half], osend.at[half])
        for kind in range(4):
            wait_sent_eight(place, send_buf.at[kind, half], send_sem.at[kind, half])
        for kind in range(3):
            wait_sent_eight(place, ret_send.at[kind, half], rsend.at[kind, half])
        for kind in (KEY, VALUE):
            for batch in range(2):
                forward(kind, half, batch).wait_send()
    for kind in range(2):
        for kg in range(4):
            for kh in range(2):
                part_copy(kind, kg, kh).wait_send()


def copy_kernel(*refs):
    for source, target in zip(refs[:3], refs[3:]):
        target[...] = source[...]


def copied(arrays):
    vmem_spec = pl.BlockSpec(memory_space=pltpu.VMEM)
    return pl.pallas_call(
        copy_kernel,
        out_shape=tuple(jax.ShapeDtypeStruct(a.shape, a.dtype) for a in arrays),
        in_specs=[vmem_spec] * 3,
        out_specs=(vmem_spec,) * 3,
        name="results",
    )(*arrays)


def on_device(tokens, segments, w_in, w_out, grad_out):
    any_spec = pl.BlockSpec(memory_space=pl.ANY)
    vmem_spec = pl.BlockSpec(memory_space=pltpu.VMEM)
    dma = pltpu.SemaphoreType.DMA
    vmem = pltpu.VMEM
    tiles = len(TILES)
    results = pl.pallas_call(
        layer_kernel,
        out_shape=(
            jax.ShapeDtypeStruct((ROWS, D), BF16),
            jax.ShapeDtypeStruct((ROWS, D), BF16),
            jax.ShapeDtypeStruct((8, D), F32),
        ),
        in_specs=[any_spec, vmem_spec, any_spec, any_spec, any_spec],
        out_specs=(vmem_spec, vmem_spec, vmem_spec),
        scratch_shapes=[
            vmem((ROWS, D), BF16),
            vmem((8, ROWS, D), BF16),
            vmem((D, 4 * D), BF16),
            vmem((D, D), BF16),
            vmem((ROWS, D), BF16),
            vmem((ROWS, 4 * D), F32),
            vmem((ROWS, D), BF16),
            vmem((ROWS, D), F32),
            vmem((1, 256), jnp.int32),
            vmem((2, 8, 1, 256), jnp.int32),
            vmem((2, 4, G, 128), BF16),
            vmem((2, 2, G, 128), BF16),
            vmem((4, 2, HEADS, HALF, HEAD), BF16),
            vmem((2, 2, 8, HALF, HEAD), BF16),
            vmem((2, 2, 8, HALF, HEAD), BF16),
            vmem((2, 8, HALF, HEAD), BF16),
            vmem((2, 8, HALF, HEAD), BF16),
            vmem((tiles, G, G), BF16),
            vmem((tiles, G, G), BF16),
            vmem((2, 4, HEAD, G), BF16),
            vmem((2, 4, HEAD, G), BF16),
            vmem((2, 2, HEAD, G), F32),
            vmem((2, 2, HEAD, G), BF16),
            vmem((2, 8, HALF, HEAD), BF16),
            vmem((2, HEADS, HALF, HEAD), BF16),
            vmem((8, 1, 256), F32),
            vmem((HEADS, 1, 256), F32),
            vmem((HEADS, 2, 8, G), F32),
            vmem((2, 2, HEAD, G), BF16),
            vmem((2, 2, HEAD, G), F32),
            vmem((2, 4, G, HEAD), F32),
            vmem((2, 2, ROWS, HEAD), F32),
            vmem((2, 4, 2, 2, HALF, HEAD), F32),
            vmem((2, 4, 2, 2, HALF, HEAD), BF16),
            vmem((2, 4, 2, 2, HALF, HEAD), BF16),
            vmem((3, 2, 8, HALF, HEAD), BF16),
            vmem((3, 2, HEADS, HALF, HEAD), BF16),
            vmem((ROWS, D), F32),
            vmem((ROWS, D), BF16),
            vmem((ROWS, D), BF16),
            vmem((8, ROWS, 128), BF16),
            vmem((CTX, 64, 128), F32),
            vmem((CTX, 64, 128), BF16),
            vmem((CTX - 1, 64, 128), BF16),
            vmem((8, 128, 128), BF16),
            vmem((8, 128, 128), BF16),
            dma((3,)), dma((8,)),
            dma, dma, dma, dma,
            dma((4, 2)), dma((4, 2, 2)), dma((2, 2, 2)), dma((2, 2, 2)),
            dma((2,)), dma((2,)), dma, dma,
            dma((2,)), dma((2,)),
            dma((2, 4, 2)), dma((2, 4, 2)), dma((3, 2)), dma((3, 2)),
            dma((3,)), dma((3,)), dma((4,)), dma((4,)),
            dma, dma, dma, dma,
            dma, dma,
        ],
        compiler_params=pltpu.CompilerParams(
            collective_id=0, has_side_effects=True, vmem_limit_bytes=VMEM_LIMIT
        ),
        name="layer",
    )(tokens, segments, w_in, w_out, grad_out)
    return copied(results)


def solution(mesh):
    return jax.shard_map(
        on_device,
        mesh=mesh,
        in_specs=(P(("dp", "ctx"), None), P("dp", "ctx"), P(), P(), P(("dp", "ctx"), None)),
        out_specs=(P(("dp", "ctx"), None), P(("dp", "ctx"), None), P(("dp", "ctx"), None)),
        check_vma=False,
    )
```
